256 devices in a mesh: space: 16 (over z, core), ray: 16 (over x, y).
Axes of the slice: x: 4, y: 4, z: 8, core: 2. Of those that a mesh axis runs over, the one named last changes fastest.
Arguments:
- grid_table: bfloat16 [16, 4096, 256], P('space'), may hold values from -6 to 6
- weights: bfloat16 [16, 4, 256, 256], P('space'), may hold values from -0.375 to 0.375
- biases: float32 [16, 4, 256], P('space'), may hold values from -1.5 to 1.5
- density_head: float32 [16, 256], P('space'), may hold values from -0.375 to 0.375
- sample_cells: int32 [16, 8192, 8], P('space', 'ray'), may hold values from 0 to 4095
- sample_counts: int32 [8192, 16], P('ray', 'space'), may hold values from 0 to 8
- ray_order: int32 [8192, 16], P('ray'), may hold values from 0 to 15, each once within a row
- cotangent: float32 [8192, 256], P('ray'), may hold values from -6 to 6
Outputs:
- composite: float32 [8192, 256], P(('ray', 'space'))
- weight_grads: float32 [16, 4, 256, 256], P('space')
- bias_grads: float32 [16, 4, 256], P('space')
- head_grads: float32 [16, 256], P('space')
The draws below stay inside these ranges and needn't reach their ends.
Inputs may be any that keep to these rules, and one draw needn't show every extreme that they name: `ray_order`: each row is a permutation of 0 .. 15: the order in which the ray meets the partitions. `sample_counts`: A count of 0 means that the ray does not touch the partition.
All inputs are finite; a program needn't handle non-finite values.
Results may differ from the reference program's by a relative error of at most 0.0065.
The reference program's roundings to bfloat16 on the way count: a program that leaves them out, or rounds other values in their place, can miss the bound.
Values sent between devices are 32-bit elements; how exact they have to be, the bound alone decides.
A program may use at most 128 MiB of HBM per device.

```python
import jax
import jax.numpy as jnp
from jax import lax

W = 256
LAYERS = 4
SAMPLES = 8
CELLS = 4096
PARTS_SIZE = 16
RAYS = 8192


def with_ends(drawn, stream_key, smallest, top_value):
    dims = drawn.shape
    place = [jax.random.randint(jax.random.fold_in(stream_key, axis), (), 0, dims[axis]) for axis in range(len(dims))]
    drawn = drawn.at[tuple(place)].set(smallest)
    longest = dims.index(max(dims))
    place[longest] = (place[longest] + 1) % dims[longest]
    return drawn.at[tuple(place)].set(top_value)


def steps_of(key, dims, pieces, low, top_value):
    def one(axis_at, blocks):
        heights = jax.random.uniform(jax.random.fold_in(jax.random.fold_in(key, 6), axis_at), (blocks,), jnp.float32, low / len(pieces), top_value / len(pieces))
        return jnp.repeat(jnp.exp(heights), dims[axis_at] // blocks).reshape((-1,) + (1,) * (len(dims) - axis_at - 1))

    loudness = one(*pieces[0])
    for cut in pieces[1:]:
        loudness = loudness * one(*cut)
    return loudness


def normal_values(own_key, extent, scale, reach, pieces=(), held_as=jnp.bfloat16):
    array = jax.random.normal(own_key, extent, jnp.float32) * scale
    if len(pieces) > 0:
        array = steps_of(own_key, extent, pieces, -0.22, 0.18) * array
    return jnp.clip(array, min=-reach, max=reach).astype(held_as)


def setup_inputs(seed: int = 0) -> dict:
    seeds = jax.random.split(jax.random.key(seed), 9)
    grid_table = normal_values(seeds[0], (PARTS_SIZE, CELLS, W), 1.0, 6.0, ((0, 16),))
    weights = normal_values(seeds[1], (PARTS_SIZE, LAYERS, W, W), W ** -0.5, 0.375, ((0, 16),))
    biases = normal_values(seeds[2], (PARTS_SIZE, LAYERS, W), 0.3, 1.5, ((0, 16),), jnp.float32)
    density_head = normal_values(seeds[3], (PARTS_SIZE, W), W ** -0.5, 0.375, ((0, 16),), jnp.float32)
    sample_cells = with_ends(jax.random.randint(seeds[4], (PARTS_SIZE, RAYS, SAMPLES), 0, CELLS), jax.random.fold_in(seeds[4], 1), 0, CELLS - 1).astype(jnp.int32)
    sample_counts = with_ends(jax.random.randint(seeds[5], (RAYS, PARTS_SIZE), 0, SAMPLES + 1), jax.random.fold_in(seeds[5], 1), 0, SAMPLES).astype(jnp.int32)
    ray_order = jax.vmap(lambda own: jax.random.permutation(own, PARTS_SIZE))(jax.random.split(seeds[6], RAYS)).reshape((RAYS, PARTS_SIZE)).astype(jnp.int32)
    cotangent = normal_values(seeds[7], (RAYS, W), 1.0, 6.0, ((0, 16),), jnp.float32)
    return {"grid_table": grid_table, "weights": weights, "biases": biases, "density_head": density_head, "sample_cells": sample_cells, "sample_counts": sample_counts, "ray_order": ray_order, "cotangent": cotangent}


step_length = 0.05

def forward(table, layer_mats, layer_bias, cells):
    hidden = table[cells.reshape(-1)]
    layer_inputs = []
    pre_acts = []
    linear = None
    for layer in range(layer_mats.shape[0]):
        layer_inputs.append(hidden)
        linear = jnp.dot(hidden, layer_mats[layer], preferred_element_type=jnp.float32) + layer_bias[layer]
        pre_acts.append(linear)
        if layer + 1 < layer_mats.shape[0]:
            hidden = jax.nn.relu(linear).astype(jnp.bfloat16)
    return (layer_inputs, pre_acts, linear)

def segment(features, head, count):
    slots = count.shape[0]
    width = features.shape[1]
    samples = features.shape[0] // slots
    logits = jnp.dot(features, head, precision=lax.Precision.HIGHEST)
    density = jax.nn.softplus(logits).reshape(slots, samples)
    live = lax.iota(jnp.int32, samples)[None, :] < count[:, None]
    optical = jnp.where(live, density * step_length, jnp.float32(0.0))
    before = jnp.cumsum(optical, axis=1) - optical
    blend = jnp.exp(-before) * (1.0 - jnp.exp(-optical))
    colour = jnp.einsum('rs,rsw->rw', blend, features.reshape(slots, samples, width), precision=lax.Precision.HIGHEST)
    decay = -lax.optimization_barrier(jnp.sum(optical, axis=1))
    return (colour, decay)

def backward(layer_inputs, pre_acts, layer_mats, grad_features):
    grad_linear = grad_features
    mats = []
    offsets = []
    for layer in range(layer_mats.shape[0] - 1, -1, -1):
        grad_half = grad_linear.astype(jnp.bfloat16)
        mats.append(lax.dot_general(layer_inputs[layer], grad_half, (((0,), (0,)), ((), ())), preferred_element_type=jnp.float32))
        offsets.append(lax.optimization_barrier(jnp.sum(grad_linear, axis=0)))
        if layer > 0:
            back = lax.dot_general(grad_half, layer_mats[layer], (((1,), (1,)), ((), ())), preferred_element_type=jnp.float32)
            grad_linear = back * (pre_acts[layer - 1] > 0).astype(jnp.float32)
    return (jnp.stack(mats[::-1]), jnp.stack(offsets[::-1]))

def reference(grid_table, weights, biases, density_head, sample_cells, sample_counts, ray_order, cotangent):
    parts = grid_table.shape[0]

    def first(index):
        layer_inputs, pre_acts, features = forward(grid_table[index], weights[index], biases[index], sample_cells[index])
        return segment(features, density_head[index], sample_counts[:, index])
    colours, decays = lax.map(first, jnp.arange(parts, dtype=jnp.int32))
    products = lax.optimization_barrier(jnp.sum(colours * cotangent[None, :, :], axis=2))
    ranks = ray_order.T
    earlier = ranks[None, :, :] < ranks[:, None, :]
    later = ranks[None, :, :] > ranks[:, None, :]
    prefix = jnp.exp(lax.optimization_barrier(jnp.sum(jnp.where(earlier, decays[None, :, :], jnp.float32(0.0)), axis=1)))
    shares = prefix * products
    tails = lax.optimization_barrier(jnp.sum(jnp.where(later, shares[None, :, :], jnp.float32(0.0)), axis=1))
    composite = lax.optimization_barrier(jnp.sum(prefix[:, :, None] * colours, axis=0))

    def second(index):
        layer_inputs, pre_acts, features = forward(grid_table[index], weights[index], biases[index], sample_cells[index])
        count = sample_counts[:, index]
        outputs, pull = jax.vjp(lambda feats, head: segment(feats, head, count), features, density_head[index])
        grad_features, grad_head = pull((prefix[index][:, None] * cotangent, tails[index]))
        mats, offsets = backward(layer_inputs, pre_acts, weights[index], grad_features)
        return (mats, offsets, grad_head)
    weight_grads, bias_grads, head_grads = lax.map(second, jnp.arange(parts, dtype=jnp.int32))
    return (composite, weight_grads, bias_grads, head_grads)
```

```python
import jax
import jax.numpy as jnp
from jax import lax
from jax.experimental import pallas as pl
from jax.experimental.pallas import tpu as pltpu
from jax.sharding import PartitionSpec as P

MESH = pl.DeviceIdType.MESH
f32 = jnp.float32
bf16 = jnp.bfloat16

STEP = 0.05
W = 256
LAYERS = 4
SLOTS = 8
CELLS = 4096
LANES = 128
RAYS = 512
GROUPS = RAYS // LANES
GROUP = SLOTS * LANES
SAMPLES = RAYS * SLOTS
WIDE = 2
CHUNKS = GROUPS // WIDE
CHUNK = WIDE * GROUP
PARTS = 16
SIDE = 4
BLOCK = W // 2 // SIDE
UNROLL = 32


def dot(a, b, ca, cb):
    return lax.dot_general(a, b, (((ca,), (cb,)), ((), ())), preferred_element_type=f32)


def scan_down(v, row):
    for k in (1, 2, 4):
        v = v + jnp.where(row >= k, pltpu.roll(v, k, 0), 0.0)
    return v


def scan_up(v, row):
    for k in (1, 2, 4):
        v = v + jnp.where(row < SLOTS - k, pltpu.roll(v, SLOTS - k, 0), 0.0)
    return v


def kernel(
    cells, table, w, bias, head, counts, ranks, cot,
    comp_out, dw_out, bias_out, head_out,
    table32, rows32, x16, wt, cols, cot_t, hid, feat, grad, seg, colour, colour_rows,
    packed, gathered, comp_in, dw, col_sums, small, small_x, small_y,
    red, in1, in2,
    ag_send, ag_recv, comp_send, comp_recv, sends, recvs, small_send, small_recv,
):
    space = lax.axis_index("space")
    ray = lax.axis_index("ray")
    spot = (ray // SIDE, ray % SIDE)

    def ray_peer(axis, d):
        there = lax.rem(spot[axis] + d, SIDE)
        return there, {"ray": there * SIDE + spot[1] if axis == 0 else spot[0] * SIDE + there}

    barrier = pltpu.get_barrier_semaphore()
    for d in range(1, PARTS):
        pl.semaphore_signal(
            barrier, inc=1, device_id={"space": lax.rem(space + d, PARTS)}, device_id_type=MESH
        )
    for axis in (0, 1):
        for d in range(1, SIDE):
            pl.semaphore_signal(
                barrier, inc=1, device_id=ray_peer(axis, d)[1], device_id_type=MESH
            )

    def widen(k, _):
        part = table[pl.ds(pl.multiple_of(k * 512, 512), 512), :].astype(f32)
        table32[pl.ds(pl.multiple_of(k * 512, 512), 512), 0, :] = part[:, :LANES]
        table32[pl.ds(pl.multiple_of(k * 512, 512), 512), 1, :] = part[:, LANES:]
        return 0

    lax.fori_loop(0, CELLS // 512, widen, 0)

    def pick(k, _):
        base = k * UNROLL
        got = [table32[cells[base + u]] for u in range(UNROLL)]
        for u in range(UNROLL):
            rows32[base + u] = got[u]
        return 0

    lax.fori_loop(0, SAMPLES // UNROLL, pick, 0)

    for layer in range(LAYERS):
        wt[layer] = w[layer].T
    cols[...] = jnp.concatenate([bias[...], head[...], jnp.zeros((3, W), f32)], axis=0).T
    cot_t[...] = cot[...].T
    slot_row = lax.broadcasted_iota(jnp.int32, (SLOTS, LANES), 0)
    ones = jnp.ones((1, LANES), f32)
    head_col = cols[:, LAYERS : LAYERS + 1] * ones

    def forward(c, _):
        start = pl.multiple_of(c * CHUNK, CHUNK)
        low = rows32[pl.ds(start, CHUNK), 0, :]
        high = rows32[pl.ds(start, CHUNK), 1, :]
        x = jnp.concatenate([low, high], axis=1).astype(bf16)
        x16[c] = x
        value = None
        for layer in range(LAYERS):
            value = dot(wt[layer], x, 1, 1 if layer == 0 else 0) + cols[:, layer : layer + 1]
            if layer + 1 < LAYERS:
                x = jnp.maximum(value, 0.0).astype(bf16)
                hid[layer, c] = x
        feat[c] = value
        return 0

    lax.fori_loop(0, CHUNKS, forward, 0)

    decay_rows, product_rows = [], []
    for g in range(GROUPS):
        lanes = slice(g * LANES, (g + 1) * LANES)
        turned = cot_t[:, lanes]
        logit, along = [], []
        for s in range(SLOTS):
            at = (g % WIDE) * GROUP + s * LANES
            f = feat[g // WIDE, :, at : at + LANES]
            logit.append(jnp.sum(f * head_col, axis=0, keepdims=True))
            along.append(jnp.sum(f * turned, axis=0, keepdims=True))
        logit = jnp.concatenate(logit, axis=0)
        along = jnp.concatenate(along, axis=0)
        live = slot_row < counts[g : g + 1, :]
        density = jnp.maximum(logit, 0.0) + jnp.log1p(jnp.exp(-jnp.abs(logit)))
        optical = jnp.where(live, density * STEP, 0.0)
        total = scan_down(optical, slot_row)
        through = jnp.exp(-(total - optical))
        past = jnp.exp(-optical)
        blend = through * (1.0 - past)
        share = blend * along
        after = scan_up(share, slot_row)
        seg[g, 0] = blend
        seg[g, 1] = along * through * past - (after - share)
        seg[g, 2] = jnp.where(live, STEP / (1.0 + jnp.exp(-logit)), 0.0)
        decay_rows.append(-total[SLOTS - 1 : SLOTS, :])
        product_rows.append(after[0:1, :])
    packed[...] = jnp.concatenate(decay_rows + product_rows, axis=0)

    pl.semaphore_wait(barrier, PARTS - 1 + 2 * (SIDE - 1))
    mine = pl.multiple_of(space * 8, 8)

    def ag_copy(d):
        return pltpu.make_async_remote_copy(
            src_ref=packed,
            dst_ref=gathered.at[pl.ds(mine, 8), :],
            send_sem=ag_send.at[d],
            recv_sem=ag_recv.at[d],
            device_id={"space": lax.rem(space + d, PARTS)},
            device_id_type=MESH,
        )

    for d in range(1, PARTS):
        ag_copy(d).start()
    gathered[pl.ds(mine, 8), :] = packed[...]

    def blend_colours(g, _):
        c = g // WIDE
        at = pl.multiple_of((g % WIDE) * GROUP, GROUP)
        blend = seg[g, 0]
        acc = None
        for s in range(SLOTS):
            term = feat[c, :, pl.ds(at + s * LANES, LANES)] * blend[s : s + 1, :]
            acc = term if acc is None else acc + term
        colour[g] = acc
        return 0

    lax.fori_loop(0, GROUPS, blend_colours, 0)
    for d in range(1, PARTS):
        ag_copy(d).wait_recv()

    decay = jnp.concatenate(
        [gathered[pl.ds(g, PARTS, stride=8), :] for g in range(GROUPS)], axis=1
    )
    product = jnp.concatenate(
        [gathered[pl.ds(GROUPS + g, PARTS, stride=8), :] for g in range(GROUPS)], axis=1
    )
    rank = ranks[...]
    earlier = jnp.zeros((PARTS, RAYS), f32)
    for q in range(PARTS):
        earlier = earlier + jnp.where(rank[q : q + 1, :] < rank, decay[q : q + 1, :], 0.0)
    prefixes = jnp.exp(earlier)
    own = lax.broadcasted_iota(jnp.int32, (PARTS, RAYS), 0) == space
    own_rank = jnp.sum(jnp.where(own, rank, 0), axis=0, keepdims=True)
    prefix = jnp.sum(jnp.where(own, prefixes, 0.0), axis=0, keepdims=True)
    tail = jnp.sum(jnp.where(rank > own_rank, prefixes * product, 0.0), axis=0, keepdims=True)

    for g in range(GROUPS):
        lanes = slice(g * LANES, (g + 1) * LANES)
        colour_rows[lanes, :] = (colour[g] * prefix[:, lanes]).T
    kept = RAYS // PARTS

    def comp_copy(d):
        there = lax.rem(space + d, PARTS)
        return pltpu.make_async_remote_copy(
            src_ref=colour_rows.at[pl.ds(pl.multiple_of(there * kept, kept), kept), :],
            dst_ref=comp_in.at[space],
            send_sem=comp_send.at[d],
            recv_sem=comp_recv.at[d],
            device_id={"space": there},
            device_id_type=MESH,
        )

    for d in range(1, PARTS):
        comp_copy(d).start()

    head_sum = jnp.zeros((W, LANES), f32)
    last_sum = jnp.zeros((W, LANES), f32)
    for g in range(GROUPS):
        lanes = slice(g * LANES, (g + 1) * LANES)
        pull = cot_t[:, lanes] * prefix[:, lanes]
        blend = seg[g, 0]
        slope = seg[g, 2] * (prefix[:, lanes] * seg[g, 1] - tail[:, lanes])
        for s in range(SLOTS):
            at = (g % WIDE) * GROUP + s * LANES
            d_logit = slope[s : s + 1, :]
            grads = pull * blend[s : s + 1, :] + head_col * d_logit
            head_sum = head_sum + feat[g // WIDE, :, at : at + LANES] * d_logit
            last_sum = last_sum + grads
            grad[g // WIDE, :, at : at + LANES] = grads.astype(bf16)
    col_sums[LAYERS] = head_sum
    col_sums[LAYERS - 1] = last_sum

    def phase1(layer, half, d):
        there, device = ray_peer(half, d)
        return pltpu.make_async_remote_copy(
            src_ref=dw.at[
                layer, pl.ds(pl.multiple_of(half * (W // 2) + there * BLOCK, BLOCK), BLOCK), :
            ],
            dst_ref=in1.at[layer, half, d],
            send_sem=sends.at[0, layer, half, d],
            recv_sem=recvs.at[0, layer, half, d],
            device_id=device,
            device_id_type=MESH,
        )

    def phase2(layer, half, d):
        return pltpu.make_async_remote_copy(
            src_ref=red.at[layer, half],
            dst_ref=in2.at[layer, half, spot[1 - half]],
            send_sem=sends.at[1, layer, half, d],
            recv_sem=recvs.at[1, layer, half, d],
            device_id=ray_peer(1 - half, d)[1],
            device_id_type=MESH,
        )

    def own_rows(half):
        return pl.ds(pl.multiple_of(half * (W // 2) + spot[half] * BLOCK, BLOCK), BLOCK)

    def phase3(layer, half, d):
        rows = dw_out.at[layer, own_rows(half), :]
        return pltpu.make_async_remote_copy(
            src_ref=rows,
            dst_ref=rows,
            send_sem=sends.at[2, layer, half, d],
            recv_sem=recvs.at[2, layer, half, d],
            device_id=ray_peer(half, d)[1],
            device_id_type=MESH,
        )

    def small_copy(axis, d):
        return pltpu.make_async_remote_copy(
            src_ref=(small, small_x.at[SIDE])[axis],
            dst_ref=(small_x, small_y)[axis].at[spot[axis]],
            send_sem=small_send.at[axis, d],
            recv_sem=small_recv.at[axis, d],
            device_id=ray_peer(axis, d)[1],
            device_id_type=MESH,
        )

    for layer in range(LAYERS - 1, -1, -1):
        for c in range(CHUNKS):
            if layer > 0:
                term = dot(hid[layer - 1, c], grad[c], 1, 1)
            else:
                term = dot(grad[c], x16[c], 1, 0)
            total = term if c == 0 else total + term
        dw[layer] = total if layer > 0 else total.T
        for d in range(1, SIDE):
            for half in (0, 1):
                phase1(layer, half, d).start()
        if layer > 0:
            def back(c, acc):
                pulled = jnp.where(hid[layer - 1, c] > 0, dot(w[layer], grad[c], 1, 0), 0.0)
                grad[c] = pulled.astype(bf16)
                for t in range(CHUNK // LANES):
                    acc = acc + pulled[:, t * LANES : (t + 1) * LANES]
                return acc

            acc = jnp.zeros((W, LANES), f32)
            for c in range(CHUNKS):
                acc = back(c, acc)
            col_sums[layer - 1] = acc

    lane = lax.broadcasted_iota(jnp.int32, (W, LANES), 1)
    gathered_cols = jnp.zeros((W, LANES), f32)
    for k in range(LAYERS + 1):
        gathered_cols = jnp.where(
            lane == k, jnp.sum(col_sums[k], axis=1, keepdims=True), gathered_cols
        )
    small[...] = gathered_cols.T[:8, :]
    for d in range(1, SIDE):
        small_copy(0, d).start()

    order = range(LAYERS - 1, -1, -1)
    for layer in order:
        for half in (0, 1):
            total = dw[layer, own_rows(half), :]
            for d in range(1, SIDE):
                phase1(layer, half, d).wait_recv()
                total = total + in1[layer, half, d]
            red[layer, half] = total
            in2[layer, half, spot[1 - half]] = total
            for d in range(1, SIDE):
                phase2(layer, half, d).start()

    small_x[spot[0]] = small[...]
    for d in range(1, SIDE):
        small_copy(0, d).wait_recv()
    small_x[SIDE] = (small_x[0] + small_x[1]) + (small_x[2] + small_x[3])
    for d in range(1, SIDE):
        small_copy(1, d).start()

    for layer in order:
        for half in (0, 1):
            for d in range(1, SIDE):
                phase2(layer, half, d).wait_recv()
            total = (in2[layer, half, 0] + in2[layer, half, 1]) + (
                in2[layer, half, 2] + in2[layer, half, 3]
            )
            dw_out[layer, own_rows(half), :] = total
            for d in range(1, SIDE):
                phase3(layer, half, d).start()

    small_y[spot[1]] = small_x[SIDE]
    for d in range(1, SIDE):
        small_copy(1, d).wait_recv()
    summed = (small_y[0] + small_y[1]) + (small_y[2] + small_y[3])
    bias_out[...] = summed[:LAYERS, :]
    head_out[...] = summed[LAYERS : LAYERS + 1, :]

    comp_in[space] = colour_rows[pl.ds(pl.multiple_of(space * kept, kept), kept), :]
    for d in range(1, PARTS):
        comp_copy(d).wait_recv()
    total = comp_in[0]
    for q in range(1, PARTS):
        total = total + comp_in[q]
    comp_out[...] = total

    for layer in order:
        for half in (0, 1):
            for d in range(1, SIDE):
                phase3(layer, half, d).wait_recv()
    for d in range(1, PARTS):
        ag_copy(d).wait_send()
        comp_copy(d).wait_send()
    for axis in (0, 1):
        for d in range(1, SIDE):
            small_copy(axis, d).wait_send()
            for layer in order:
                for phase in (phase1, phase2, phase3):
                    phase(layer, axis, d).wait_send()


def on_device(
    grid_table, weights, biases, density_head, sample_cells, sample_counts, ray_order, cotangent
):
    cells = sample_cells[0].T.reshape(SLOTS, GROUPS, LANES).transpose(1, 0, 2).reshape(SAMPLES)
    counts = sample_counts.reshape(GROUPS, LANES)
    in_vmem = pl.BlockSpec(memory_space=pltpu.VMEM)
    dma = pltpu.SemaphoreType.DMA
    composite, dw, db, dh = pl.pallas_call(
        kernel,
        out_shape=(
            jax.ShapeDtypeStruct((RAYS // PARTS, W), f32),
            jax.ShapeDtypeStruct((LAYERS, W, W), f32),
            jax.ShapeDtypeStruct((LAYERS, W), f32),
            jax.ShapeDtypeStruct((1, W), f32),
        ),
        in_specs=[pl.BlockSpec(memory_space=pltpu.SMEM)] + [in_vmem] * 7,
        out_specs=(in_vmem,) * 4,
        scratch_shapes=[
            pltpu.VMEM((CELLS, 2, LANES), f32),
            pltpu.VMEM((SAMPLES, 2, LANES), f32),
            pltpu.VMEM((CHUNKS, CHUNK, W), bf16),
            pltpu.VMEM((LAYERS, W, W), bf16),
            pltpu.VMEM((W, 8), f32),
            pltpu.VMEM((W, RAYS), f32),
            pltpu.VMEM((LAYERS - 1, CHUNKS, W, CHUNK), bf16),
            pltpu.VMEM((CHUNKS, W, CHUNK), f32),
            pltpu.VMEM((CHUNKS, W, CHUNK), bf16),
            pltpu.VMEM((GROUPS, 3, SLOTS, LANES), f32),
            pltpu.VMEM((GROUPS, W, LANES), f32),
            pltpu.VMEM((RAYS, W), f32),
            pltpu.VMEM((8, LANES), f32),
            pltpu.VMEM((PARTS * 8, LANES), f32),
            pltpu.VMEM((PARTS, RAYS // PARTS, W), f32),
            pltpu.VMEM((LAYERS, W, W), f32),
            pltpu.VMEM((LAYERS + 1, W, LANES), f32),
            pltpu.VMEM((8, W), f32),
            pltpu.VMEM((SIDE + 1, 8, W), f32),
            pltpu.VMEM((SIDE, 8, W), f32),
            pltpu.VMEM((LAYERS, 2, BLOCK, W), f32),
            pltpu.VMEM((LAYERS, 2, SIDE, BLOCK, W), f32),
            pltpu.VMEM((LAYERS, 2, SIDE, BLOCK, W), f32),
            dma((PARTS,)),
            dma((PARTS,)),
            dma((PARTS,)),
            dma((PARTS,)),
            dma((3, LAYERS, 2, SIDE)),
            dma((3, LAYERS, 2, SIDE)),
            dma((2, SIDE)),
            dma((2, SIDE)),
        ],
        compiler_params=pltpu.CompilerParams(
            collective_id=0, has_side_effects=True, vmem_limit_bytes=58 << 20
        ),
        cost_estimate=pl.CostEstimate(
            flops=22 * SAMPLES * W * W, bytes_accessed=6 << 20, transcendentals=6 * SAMPLES
        ),
    )(
        cells, grid_table[0], weights[0], biases[0], density_head, counts, ray_order.T, cotangent
    )
    return composite, dw[None], db[None], dh


def solution(mesh):
    placed = (
        P("space", None, None),
        P("space", None, None, None),
        P("space", None, None),
        P("space", None),
        P("space", "ray", None),
        P("ray", "space"),
        P("ray", None),
        P("ray", None),
    )
    return jax.shard_map(
        on_device,
        mesh=mesh,
        in_specs=placed,
        out_specs=(
            P(("ray", "space"), None),
            P("space", None, None, None),
            P("space", None, None),
            P("space", None),
        ),
        check_vma=False,
    )
```

```python
import jax
import jax.numpy as jnp
from jax import lax
from jax.experimental import pallas as pl
from jax.experimental.pallas import tpu as pltpu
from jax.sharding import PartitionSpec as P

MESH = pl.DeviceIdType.MESH
f32 = jnp.float32
bf16 = jnp.bfloat16

STEP = 0.05
W = 256
LAYERS = 4
SLOTS = 8
CELLS = 4096
LANES = 128
RAYS = 512
GROUPS = RAYS // LANES
GROUP = SLOTS * LANES
SAMPLES = RAYS * SLOTS
WIDE = 2
CHUNKS = GROUPS // WIDE
CHUNK = WIDE * GROUP
PARTS = 16
SIDE = 4
BLOCK = W // 2 // SIDE
PART = BLOCK // SIDE
UNROLL = 32


def dot(a, b, ca, cb):
    return lax.dot_general(a, b, (((ca,), (cb,)), ((), ())), preferred_element_type=f32)


def scan_down(v, row):
    for k in (1, 2, 4):
        v = v + jnp.where(row >= k, pltpu.roll(v, k, 0), 0.0)
    return v


def scan_up(v, row):
    for k in (1, 2, 4):
        v = v + jnp.where(row < SLOTS - k, pltpu.roll(v, SLOTS - k, 0), 0.0)
    return v


def kernel(
    cells, table, w, bias, head, counts, ranks, cot,
    comp_out, dw_out, bias_out, head_out,
    table32, rows32, x16, wt, cols, cot_t, hid, feat, grad, seg, colour, colour_rows,
    packed, gathered, comp_in, dw, col_sums, small, small_x, small_y,
    in1, out1, red, in2,
    ag_send, ag_recv, comp_send, comp_recv, sends, recvs, across_send, across_recv,
    small_send, small_recv,
):
    space = lax.axis_index("space")
    ray = lax.axis_index("ray")
    spot = (ray // SIDE, ray % SIDE)

    def ray_peer(axis, d):
        there = lax.rem(spot[axis] + d, SIDE)
        return there, {"ray": there * SIDE + spot[1] if axis == 0 else spot[0] * SIDE + there}

    barrier = pltpu.get_barrier_semaphore()
    for d in range(1, PARTS):
        pl.semaphore_signal(
            barrier, inc=1, device_id={"space": lax.rem(space + d, PARTS)}, device_id_type=MESH
        )
    for axis in (0, 1):
        for d in range(1, SIDE):
            pl.semaphore_signal(
                barrier, inc=1, device_id=ray_peer(axis, d)[1], device_id_type=MESH
            )

    def widen(k, _):
        part = table[pl.ds(pl.multiple_of(k * 512, 512), 512), :].astype(f32)
        table32[pl.ds(pl.multiple_of(k * 1024, 1024), 512, stride=2), :] = part[:, :LANES]
        table32[pl.ds(pl.multiple_of(k * 1024, 1024) + 1, 512, stride=2), :] = part[:, LANES:]
        return 0

    lax.fori_loop(0, CELLS // 512, widen, 0)

    def pick(k, _):
        base = k * UNROLL
        got = [
            table32[pl.ds(2 * cells[base + u], 2), :] for u in range(UNROLL)
        ]
        for u in range(UNROLL):
            rows32[pl.ds(pl.multiple_of(2 * base, 2 * UNROLL) + 2 * u, 2), :] = got[u]
        return 0

    lax.fori_loop(0, SAMPLES // UNROLL, pick, 0)

    for layer in range(LAYERS):
        wt[layer] = w[layer].T
    cols[...] = jnp.concatenate([bias[...], head[...], jnp.zeros((3, W), f32)], axis=0).T
    cot_t[...] = cot[...].T
    slot_row = lax.broadcasted_iota(jnp.int32, (SLOTS, LANES), 0)
    ones = jnp.ones((1, LANES), f32)
    head_col = cols[:, LAYERS : LAYERS + 1] * ones

    def forward(c, _):
        start = pl.multiple_of(c * 2 * CHUNK, 2 * CHUNK)
        low = rows32[pl.ds(start, CHUNK, stride=2), :]
        high = rows32[pl.ds(start + 1, CHUNK, stride=2), :]
        x = jnp.concatenate([low, high], axis=1).astype(bf16)
        x16[c] = x
        value = None
        for layer in range(LAYERS):
            value = dot(wt[layer], x, 1, 1 if layer == 0 else 0) + cols[:, layer : layer + 1]
            if layer + 1 < LAYERS:
                x = jnp.maximum(value, 0.0).astype(bf16)
                hid[layer, c] = x
        feat[c] = value
        return 0

    lax.fori_loop(0, CHUNKS, forward, 0)

    decay_rows, product_rows = [], []
    for g in range(GROUPS):
        lanes = slice(g * LANES, (g + 1) * LANES)
        turned = cot_t[:, lanes]
        logit, along = [], []
        for s in range(SLOTS):
            at = (g % WIDE) * GROUP + s * LANES
            f = feat[g // WIDE, :, at : at + LANES]
            logit.append(jnp.sum(f * head_col, axis=0, keepdims=True))
            along.append(jnp.sum(f * turned, axis=0, keepdims=True))
        logit = jnp.concatenate(logit, axis=0)
        along = jnp.concatenate(along, axis=0)
        live = slot_row < counts[g : g + 1, :]
        density = jnp.maximum(logit, 0.0) + jnp.log1p(jnp.exp(-jnp.abs(logit)))
        optical = jnp.where(live, density * STEP, 0.0)
        total = scan_down(optical, slot_row)
        through = jnp.exp(-(total - optical))
        past = jnp.exp(-optical)
        blend = through * (1.0 - past)
        share = blend * along
        after = scan_up(share, slot_row)
        seg[g, 0] = blend
        seg[g, 1] = along * through * past - (after - share)
        seg[g, 2] = jnp.where(live, STEP / (1.0 + jnp.exp(-logit)), 0.0)
        decay_rows.append(-total[SLOTS - 1 : SLOTS, :])
        product_rows.append(after[0:1, :])
    packed[...] = jnp.concatenate(decay_rows + product_rows, axis=0)

    pl.semaphore_wait(barrier, PARTS - 1 + 2 * (SIDE - 1))
    mine = pl.multiple_of(space * 8, 8)

    def ag_copy(d):
        return pltpu.make_async_remote_copy(
            src_ref=packed,
            dst_ref=gathered.at[pl.ds(mine, 8), :],
            send_sem=ag_send.at[d],
            recv_sem=ag_recv.at[d],
            device_id={"space": lax.rem(space + d, PARTS)},
            device_id_type=MESH,
        )

    for d in range(1, PARTS):
        ag_copy(d).start()
    gathered[pl.ds(mine, 8), :] = packed[...]

    def blend_colours(g, _):
        c = g // WIDE
        at = pl.multiple_of((g % WIDE) * GROUP, GROUP)
        blend = seg[g, 0]
        acc = None
        for s in range(SLOTS):
            term = feat[c, :, pl.ds(at + s * LANES, LANES)] * blend[s : s + 1, :]
            acc = term if acc is None else acc + term
        colour[g] = acc
        return 0

    lax.fori_loop(0, GROUPS, blend_colours, 0)
    for d in range(1, PARTS):
        ag_copy(d).wait_recv()

    decay = jnp.concatenate(
        [gathered[pl.ds(g, PARTS, stride=8), :] for g in range(GROUPS)], axis=1
    )
    product = jnp.concatenate(
        [gathered[pl.ds(GROUPS + g, PARTS, stride=8), :] for g in range(GROUPS)], axis=1
    )
    rank = ranks[...]
    earlier = jnp.zeros((PARTS, RAYS), f32)
    for q in range(PARTS):
        earlier = earlier + jnp.where(rank[q : q + 1, :] < rank, decay[q : q + 1, :], 0.0)
    prefixes = jnp.exp(earlier)
    own = lax.broadcasted_iota(jnp.int32, (PARTS, RAYS), 0) == space
    own_rank = jnp.sum(jnp.where(own, rank, 0), axis=0, keepdims=True)
    prefix = jnp.sum(jnp.where(own, prefixes, 0.0), axis=0, keepdims=True)
    tail = jnp.sum(jnp.where(rank > own_rank, prefixes * product, 0.0), axis=0, keepdims=True)

    for g in range(GROUPS):
        lanes = slice(g * LANES, (g + 1) * LANES)
        colour_rows[lanes, :] = (colour[g] * prefix[:, lanes]).T
    kept = RAYS // PARTS

    def comp_copy(d):
        there = lax.rem(space + d, PARTS)
        return pltpu.make_async_remote_copy(
            src_ref=colour_rows.at[pl.ds(pl.multiple_of(there * kept, kept), kept), :],
            dst_ref=comp_in.at[space],
            send_sem=comp_send.at[d],
            recv_sem=comp_recv.at[d],
            device_id={"space": there},
            device_id_type=MESH,
        )

    for d in range(1, PARTS):
        comp_copy(d).start()

    head_sum = jnp.zeros((W, LANES), f32)
    last_sum = jnp.zeros((W, LANES), f32)
    for g in range(GROUPS):
        lanes = slice(g * LANES, (g + 1) * LANES)
        pull = cot_t[:, lanes] * prefix[:, lanes]
        blend = seg[g, 0]
        slope = seg[g, 2] * (prefix[:, lanes] * seg[g, 1] - tail[:, lanes])
        for s in range(SLOTS):
            at = (g % WIDE) * GROUP + s * LANES
            d_logit = slope[s : s + 1, :]
            grads = pull * blend[s : s + 1, :] + head_col * d_logit
            head_sum = head_sum + feat[g // WIDE, :, at : at + LANES] * d_logit
            last_sum = last_sum + grads
            grad[g // WIDE, :, at : at + LANES] = grads.astype(bf16)
    col_sums[LAYERS] = head_sum
    col_sums[LAYERS - 1] = last_sum

    def block_rows(half, d):
        there = lax.rem(spot[half] + d + SIDE, SIDE)
        return pl.ds(pl.multiple_of(half * (W // 2) + there * BLOCK, BLOCK), BLOCK)

    def part_rows(half, d):
        return pl.ds(pl.multiple_of(lax.rem(spot[1 - half] + d, SIDE) * PART, PART), PART)

    sides = (pl.ds(0, LANES), pl.ds(LANES, LANES))
    ways = (1, -1)

    def step_copy(src, dst, layer, half, way, kind):
        return pltpu.make_async_remote_copy(
            src_ref=src,
            dst_ref=dst,
            send_sem=sends.at[layer, half, way, kind],
            recv_sem=recvs.at[layer, half, way, kind],
            device_id=ray_peer(half, ways[way] + SIDE)[1],
            device_id_type=MESH,
        )

    def far(layer, half, way):
        src = dw.at[layer, block_rows(half, 2), sides[way]]
        return step_copy(src, in1.at[layer, half, way, 0], layer, half, way, 0)

    def near(layer, half, way):
        src = dw.at[layer, block_rows(half, ways[way]), sides[1 - way]]
        return step_copy(src, in1.at[layer, half, way, 1], layer, half, way, 1)

    def joint(layer, half, way):
        src = out1.at[layer, half, way]
        return step_copy(src, in1.at[layer, half, way, 2], layer, half, way, 2)

    def give(layer, half, way):
        rows = dw_out.at[layer, block_rows(half, 0), :]
        return step_copy(rows, rows, layer, half, way, 3)

    def forward_on(layer, half, way):
        rows = dw_out.at[layer, block_rows(half, -ways[way]), sides[way]]
        return step_copy(rows, rows, layer, half, way, 4)

    def across_copy(src, dst, layer, half, d, kind):
        return pltpu.make_async_remote_copy(
            src_ref=src,
            dst_ref=dst,
            send_sem=across_send.at[layer, half, kind, d],
            recv_sem=across_recv.at[layer, half, kind, d],
            device_id=ray_peer(1 - half, d)[1],
            device_id_type=MESH,
        )

    def scatter(layer, half, d):
        src = red.at[layer, half, part_rows(half, d), :]
        return across_copy(src, in2.at[layer, half, d], layer, half, d, 0)

    def own_part(half):
        start = half * (W // 2) + spot[half] * BLOCK + spot[1 - half] * PART
        return pl.ds(pl.multiple_of(start, PART), PART)

    def spread(layer, half, d):
        rows = dw_out.at[layer, own_part(half), :]
        return across_copy(rows, rows, layer, half, d, 1)

    def reduce_stage(stage, layer):
        for half in (0, 1):
            if stage == 0:
                for copy in (far, near):
                    for way in (0, 1):
                        copy(layer, half, way).start()
            if stage == 1:
                for way in (0, 1):
                    far(layer, half, way).wait_recv()
                    out1[layer, half, way] = (
                        in1[layer, half, way, 0] + dw[layer, block_rows(half, ways[way]), sides[way]]
                    )
                    joint(layer, half, way).start()
            if stage == 2:
                for way in (0, 1):
                    near(layer, half, 1 - way).wait_recv()
                    joint(layer, half, way).wait_recv()
                    red[layer, half, :, sides[way]] = (
                        dw[layer, block_rows(half, 0), sides[way]]
                        + in1[layer, half, 1 - way, 1]
                        + in1[layer, half, way, 2]
                    )
                for d in range(1, SIDE):
                    scatter(layer, half, d).start()
            if stage == 3:
                total = red[layer, half, part_rows(half, 0), :]
                for d in range(1, SIDE):
                    scatter(layer, half, d).wait_recv()
                    total = total + in2[layer, half, d]
                dw_out[layer, own_part(half), :] = total
                for d in range(1, SIDE):
                    spread(layer, half, d).start()
            if stage == 4:
                for d in range(1, SIDE):
                    spread(layer, half, d).wait_recv()
                for way in (0, 1):
                    give(layer, half, way).start()
            if stage == 5:
                for way in (0, 1):
                    give(layer, half, way).wait_recv()
                    forward_on(layer, half, way).start()
            if stage == 6:
                for way in (0, 1):
                    forward_on(layer, half, way).wait_recv()
            if stage == 7:
                for way in (0, 1):
                    for copy in (far, near, joint, give, forward_on):
                        copy(layer, half, way).wait_send()
                for d in range(1, SIDE):
                    scatter(layer, half, d).wait_send()
                    spread(layer, half, d).wait_send()

    def small_copy(axis, d):
        return pltpu.make_async_remote_copy(
            src_ref=(small, small_x.at[SIDE])[axis],
            dst_ref=(small_x, small_y)[axis].at[spot[axis]],
            send_sem=small_send.at[axis, d],
            recv_sem=small_recv.at[axis, d],
            device_id=ray_peer(axis, d)[1],
            device_id_type=MESH,
        )

    for layer in range(LAYERS - 1, -1, -1):
        for c in range(CHUNKS):
            if layer > 0:
                term = dot(hid[layer - 1, c], grad[c], 1, 1)
            else:
                term = dot(grad[c], x16[c], 1, 0)
            total = term if c == 0 else total + term
        dw[layer] = total if layer > 0 else total.T
        reduce_stage(0, layer)
        if layer + 1 < LAYERS:
            reduce_stage(1, layer + 1)
        if layer > 0:
            def back(c, acc):
                pulled = jnp.where(hid[layer - 1, c] > 0, dot(w[layer], grad[c], 1, 0), 0.0)
                grad[c] = pulled.astype(bf16)
                for t in range(CHUNK // LANES):
                    acc = acc + pulled[:, t * LANES : (t + 1) * LANES]
                return acc

            acc = jnp.zeros((W, LANES), f32)
            for c in range(CHUNKS):
                acc = back(c, acc)
            col_sums[layer - 1] = acc

    lane = lax.broadcasted_iota(jnp.int32, (W, LANES), 1)
    gathered_cols = jnp.zeros((W, LANES), f32)
    for k in range(LAYERS + 1):
        gathered_cols = jnp.where(
            lane == k, jnp.sum(col_sums[k], axis=1, keepdims=True), gathered_cols
        )
    small[...] = gathered_cols.T[:8, :]
    for d in range(1, SIDE):
        small_copy(0, d).start()

    for wave in range(2, LAYERS + 6):
        for stage in range(6, 0, -1):
            layer = LAYERS - 1 - (wave - stage)
            if 0 <= layer < LAYERS and not (stage == 1 and layer > 0):
                reduce_stage(stage, layer)
        if wave == 2:
            small_x[spot[0]] = small[...]
            for d in range(1, SIDE):
                small_copy(0, d).wait_recv()
            small_x[SIDE] = (small_x[0] + small_x[1]) + (small_x[2] + small_x[3])
            for d in range(1, SIDE):
                small_copy(1, d).start()
        if wave == 4:
            small_y[spot[1]] = small_x[SIDE]
            for d in range(1, SIDE):
                small_copy(1, d).wait_recv()
            summed = (small_y[0] + small_y[1]) + (small_y[2] + small_y[3])
            bias_out[...] = summed[:LAYERS, :]
            head_out[...] = summed[LAYERS : LAYERS + 1, :]
        if wave == 6:
            comp_in[space] = colour_rows[pl.ds(pl.multiple_of(space * kept, kept), kept), :]
            for d in range(1, PARTS):
                comp_copy(d).wait_recv()
            total = comp_in[0]
            for q in range(1, PARTS):
                total = total + comp_in[q]
            comp_out[...] = total

    for d in range(1, PARTS):
        ag_copy(d).wait_send()
        comp_copy(d).wait_send()
    for axis in (0, 1):
        for d in range(1, SIDE):
            small_copy(axis, d).wait_send()
    for layer in range(LAYERS):
        reduce_stage(7, layer)


def hand_out(*refs):
    sems = refs[8]
    copies = [pltpu.make_async_copy(refs[k], refs[4 + k], sems.at[k]) for k in (1, 0, 2, 3)]
    for copy in copies:
        copy.start()
    for copy in copies:
        copy.wait()


def on_device(
    grid_table, weights, biases, density_head, sample_cells, sample_counts, ray_order, cotangent
):
    cells = sample_cells[0].T.reshape(SLOTS, GROUPS, LANES).transpose(1, 0, 2).reshape(SAMPLES)
    counts = sample_counts.reshape(GROUPS, LANES)
    in_vmem = pl.BlockSpec(memory_space=pltpu.VMEM)
    dma = pltpu.SemaphoreType.DMA
    composite, dw, db, dh = pl.pallas_call(
        kernel,
        out_shape=(
            pltpu.VMEM((RAYS // PARTS, W), f32),
            pltpu.VMEM((LAYERS, W, W), f32),
            pltpu.VMEM((LAYERS, W), f32),
            pltpu.VMEM((1, W), f32),
        ),
        in_specs=[pl.BlockSpec(memory_space=pltpu.SMEM)] + [in_vmem] * 7,
        out_specs=(in_vmem,) * 4,
        scratch_shapes=[
            pltpu.VMEM((2 * CELLS, LANES), f32),
            pltpu.VMEM((2 * SAMPLES, LANES), f32),
            pltpu.VMEM((CHUNKS, CHUNK, W), bf16),
            pltpu.VMEM((LAYERS, W, W), bf16),
            pltpu.VMEM((W, 8), f32),
            pltpu.VMEM((W, RAYS), f32),
            pltpu.VMEM((LAYERS - 1, CHUNKS, W, CHUNK), bf16),
            pltpu.VMEM((CHUNKS, W, CHUNK), f32),
            pltpu.VMEM((CHUNKS, W, CHUNK), bf16),
            pltpu.VMEM((GROUPS, 3, SLOTS, LANES), f32),
            pltpu.VMEM((GROUPS, W, LANES), f32),
            pltpu.VMEM((RAYS, W), f32),
            pltpu.VMEM((8, LANES), f32),
            pltpu.VMEM((PARTS * 8, LANES), f32),
            pltpu.VMEM((PARTS, RAYS // PARTS, W), f32),
            pltpu.VMEM((LAYERS, W, W), f32),
            pltpu.VMEM((LAYERS + 1, W, LANES), f32),
            pltpu.VMEM((8, W), f32),
            pltpu.VMEM((SIDE + 1, 8, W), f32),
            pltpu.VMEM((SIDE, 8, W), f32),
            pltpu.VMEM((LAYERS, 2, 2, 3, BLOCK, LANES), f32),
            pltpu.VMEM((LAYERS, 2, 2, BLOCK, LANES), f32),
            pltpu.VMEM((LAYERS, 2, BLOCK, W), f32),
            pltpu.VMEM((LAYERS, 2, SIDE, PART, W), f32),
            dma((PARTS,)),
            dma((PARTS,)),
            dma((PARTS,)),
            dma((PARTS,)),
            dma((LAYERS, 2, 2, 5)),
            dma((LAYERS, 2, 2, 5)),
            dma((LAYERS, 2, 2, SIDE)),
            dma((LAYERS, 2, 2, SIDE)),
            dma((2, SIDE)),
            dma((2, SIDE)),
        ],
        compiler_params=pltpu.CompilerParams(
            collective_id=0, has_side_effects=True, vmem_limit_bytes=58 << 20
        ),
        cost_estimate=pl.CostEstimate(
            flops=22 * SAMPLES * W * W, bytes_accessed=6 << 20, transcendentals=6 * SAMPLES
        ),
    )(
        cells, grid_table[0], weights[0], biases[0], density_head, counts, ray_order.T, cotangent
    )
    parts = (composite, dw, db, dh)
    composite, dw, db, dh = pl.pallas_call(
        hand_out,
        out_shape=tuple(jax.ShapeDtypeStruct(p.shape, f32) for p in parts),
        in_specs=[in_vmem] * 4,
        out_specs=(pl.BlockSpec(memory_space=pl.ANY),) * 4,
        scratch_shapes=[dma((4,))],
    )(*(pltpu.with_memory_space_constraint(p, pltpu.VMEM) for p in parts))
    return composite, dw[None], db[None], dh


def solution(mesh):
    placed = (
        P("space", None, None),
        P("space", None, None, None),
        P("space", None, None),
        P("space", None),
        P("space", "ray", None),
        P("ray", "space"),
        P("ray", None),
        P("ray", None),
    )
    return jax.shard_map(
        on_device,
        mesh=mesh,
        in_specs=placed,
        out_specs=(
            P(("ray", "space"), None),
            P("space", None, None, None),
            P("space", None, None),
            P("space", None),
        ),
        check_vma=False,
    )
```

```python
import jax
import jax.numpy as jnp
from jax import lax
from jax.experimental import pallas as pl
from jax.experimental.pallas import tpu as pltpu
from jax.sharding import PartitionSpec as P

MESH = pl.DeviceIdType.MESH
f32 = jnp.float32
bf16 = jnp.bfloat16

STEP = 0.05
W = 256
LAYERS = 4
SLOTS = 8
CELLS = 4096
LANES = 128
RAYS = 512
GROUPS = RAYS // LANES
GROUP = SLOTS * LANES
SAMPLES = RAYS * SLOTS
WIDE = 2
CHUNKS = GROUPS // WIDE
CHUNK = WIDE * GROUP
PARTS = 16
SIDE = 4
BLOCK = W // 2 // SIDE
UNROLL = 32
PIECES = 4
PIECE = CELLS // PIECES


def dot(a, b, ca, cb):
    return lax.dot_general(a, b, (((ca,), (cb,)), ((), ())), preferred_element_type=f32)


def scan_down(v, row):
    for k in (1, 2, 4):
        v = v + jnp.where(row >= k, pltpu.roll(v, k, 0), 0.0)
    return v


def scan_up(v, row):
    for k in (1, 2, 4):
        v = v + jnp.where(row < SLOTS - k, pltpu.roll(v, SLOTS - k, 0), 0.0)
    return v


def kernel(
    cells, table_hbm, w_hbm, bias, head, counts, ranks, cot_hbm,
    comp_out, dw_out, bias_out, head_out,
    table, w, cot, fetch, table32, rows32, x16, wt, cols, cot_t, hid, feat, grad, seg, colour, colour_rows,
    packed, gathered, comp_in, dw, col_sums, small, small_x, small_y,
    red, in1, in2,
    ag_send, ag_recv, comp_send, comp_recv, sends, recvs, small_send, small_recv,
):
    def piece(k):
        rows = pl.ds(k * PIECE, PIECE)
        return pltpu.make_async_copy(table_hbm.at[rows, :], table.at[rows, :], fetch.at[k])

    others = (
        pltpu.make_async_copy(w_hbm, w, fetch.at[PIECES]),
        pltpu.make_async_copy(cot_hbm, cot, fetch.at[PIECES + 1]),
    )
    for k in range(PIECES):
        piece(k).start()
    for copy in others:
        copy.start()
    space = lax.axis_index("space")
    ray = lax.axis_index("ray")
    spot = (ray // SIDE, ray % SIDE)

    def ray_peer(axis, d):
        there = lax.rem(spot[axis] + d, SIDE)
        return there, {"ray": there * SIDE + spot[1] if axis == 0 else spot[0] * SIDE + there}

    barrier = pltpu.get_barrier_semaphore()
    for d in range(1, PARTS):
        pl.semaphore_signal(
            barrier, inc=1, device_id={"space": lax.rem(space + d, PARTS)}, device_id_type=MESH
        )
    for axis in (0, 1):
        for d in range(1, SIDE):
            pl.semaphore_signal(
                barrier, inc=1, device_id=ray_peer(axis, d)[1], device_id_type=MESH
            )

    for k in range(PIECES):
        piece(k).wait()

        def widen(t, _):
            start = pl.multiple_of(k * PIECE + t * 512, 512)
            part = table[pl.ds(start, 512), :].astype(f32)
            table32[pl.ds(pl.multiple_of(2 * start, 1024), 512, stride=2), :] = part[:, :LANES]
            table32[pl.ds(pl.multiple_of(2 * start, 1024) + 1, 512, stride=2), :] = part[:, LANES:]
            return 0

        lax.fori_loop(0, PIECE // 512, widen, 0)

    def pick(k, _):
        base = k * UNROLL
        got = [
            table32[pl.ds(2 * cells[base + u], 2), :] for u in range(UNROLL)
        ]
        for u in range(UNROLL):
            rows32[pl.ds(pl.multiple_of(2 * base, 2 * UNROLL) + 2 * u, 2), :] = got[u]
        return 0

    lax.fori_loop(0, GROUP // UNROLL, pick, 0)

    for copy in others:
        copy.wait()
    for layer in range(LAYERS):
        wt[layer] = w[layer].T
    cols[...] = jnp.concatenate([bias[...], head[...], jnp.zeros((3, W), f32)], axis=0).T
    cot_t[...] = cot[...].T
    slot_row = lax.broadcasted_iota(jnp.int32, (SLOTS, LANES), 0)
    ones = jnp.ones((1, LANES), f32)
    head_col = cols[:, LAYERS : LAYERS + 1] * ones

    def forward(g, more):
        start = pl.multiple_of(g * 2 * GROUP, 2 * GROUP)
        low = rows32[pl.ds(start, GROUP, stride=2), :]
        high = rows32[pl.ds(start + 1, GROUP, stride=2), :]
        x = jnp.concatenate([low, high], axis=1).astype(bf16)
        half = pl.ds(pl.multiple_of((g % WIDE) * GROUP, GROUP), GROUP)
        x16[g // WIDE, half, :] = x
        value = None
        for layer in range(LAYERS):
            if more:
                for u in range(layer * GROUP // LAYERS, (layer + 1) * GROUP // LAYERS):
                    row = table32[pl.ds(2 * cells[(g + 1) * GROUP + u], 2), :]
                    rows32[pl.ds(pl.multiple_of((g + 1) * 2 * GROUP, 2 * GROUP) + 2 * u, 2), :] = row
            value = dot(wt[layer], x, 1, 1 if layer == 0 else 0) + cols[:, layer : layer + 1]
            if layer + 1 < LAYERS:
                x = jnp.maximum(value, 0.0).astype(bf16)
                hid[layer, g // WIDE, :, half] = x
        feat[g // WIDE, :, half] = value

    def segment(g):
        turned = cot_t[:, pl.ds(pl.multiple_of(g * LANES, LANES), LANES)]
        logit, along = [], []
        for s in range(SLOTS):
            at = pl.multiple_of((g % WIDE) * GROUP, GROUP) + s * LANES
            f = feat[g // WIDE, :, pl.ds(at, LANES)]
            logit.append(jnp.sum(f * head_col, axis=0, keepdims=True))
            along.append(jnp.sum(f * turned, axis=0, keepdims=True))
        logit = jnp.concatenate(logit, axis=0)
        along = jnp.concatenate(along, axis=0)
        live = slot_row < counts[pl.ds(g, 1), :]
        density = jnp.maximum(logit, 0.0) + jnp.log1p(jnp.exp(-jnp.abs(logit)))
        optical = jnp.where(live, density * STEP, 0.0)
        total = scan_down(optical, slot_row)
        through = jnp.exp(-(total - optical))
        past = jnp.exp(-optical)
        blend = through * (1.0 - past)
        share = blend * along
        after = scan_up(share, slot_row)
        seg[g, 0] = blend
        seg[g, 1] = along * through * past - (after - share)
        seg[g, 2] = jnp.where(live, STEP / (1.0 + jnp.exp(-logit)), 0.0)
        packed[pl.ds(g, 1), :] = -total[SLOTS - 1 : SLOTS, :]
        packed[pl.ds(GROUPS + g, 1), :] = after[0:1, :]

    for g in range(GROUPS):
        forward(g, g + 1 < GROUPS)
        if g > 0:
            segment(g - 1)
    segment(GROUPS - 1)

    pl.semaphore_wait(barrier, PARTS - 1 + 2 * (SIDE - 1))
    mine = pl.multiple_of(space * 8, 8)

    def ag_copy(d):
        return pltpu.make_async_remote_copy(
            src_ref=packed,
            dst_ref=gathered.at[pl.ds(mine, 8), :],
            send_sem=ag_send.at[d],
            recv_sem=ag_recv.at[d],
            device_id={"space": lax.rem(space + d, PARTS)},
            device_id_type=MESH,
        )

    for d in range(1, PARTS):
        ag_copy(d).start()
    gathered[pl.ds(mine, 8), :] = packed[...]

    def blend_colours(g, _):
        c = g // WIDE
        at = pl.multiple_of((g % WIDE) * GROUP, GROUP)
        blend = seg[g, 0]
        acc = None
        for s in range(SLOTS):
            term = feat[c, :, pl.ds(at + s * LANES, LANES)] * blend[s : s + 1, :]
            acc = term if acc is None else acc + term
        colour[g] = acc
        return 0

    lax.fori_loop(0, GROUPS, blend_colours, 0)
    for d in range(1, PARTS):
        ag_copy(d).wait_recv()

    decay = jnp.concatenate(
        [gathered[pl.ds(g, PARTS, stride=8), :] for g in range(GROUPS)], axis=1
    )
    product = jnp.concatenate(
        [gathered[pl.ds(GROUPS + g, PARTS, stride=8), :] for g in range(GROUPS)], axis=1
    )
    rank = ranks[...]
    earlier = jnp.zeros((PARTS, RAYS), f32)
    for q in range(PARTS):
        earlier = earlier + jnp.where(rank[q : q + 1, :] < rank, decay[q : q + 1, :], 0.0)
    prefixes = jnp.exp(earlier)
    own = lax.broadcasted_iota(jnp.int32, (PARTS, RAYS), 0) == space
    own_rank = jnp.sum(jnp.where(own, rank, 0), axis=0, keepdims=True)
    prefix = jnp.sum(jnp.where(own, prefixes, 0.0), axis=0, keepdims=True)
    tail = jnp.sum(jnp.where(rank > own_rank, prefixes * product, 0.0), axis=0, keepdims=True)

    for g in range(GROUPS):
        lanes = slice(g * LANES, (g + 1) * LANES)
        colour_rows[lanes, :] = (colour[g] * prefix[:, lanes]).T
    kept = RAYS // PARTS

    def comp_copy(d):
        there = lax.rem(space + d, PARTS)
        return pltpu.make_async_remote_copy(
            src_ref=colour_rows.at[pl.ds(pl.multiple_of(there * kept, kept), kept), :],
            dst_ref=comp_in.at[space],
            send_sem=comp_send.at[d],
            recv_sem=comp_recv.at[d],
            device_id={"space": there},
            device_id_type=MESH,
        )

    for d in range(1, PARTS):
        comp_copy(d).start()

    head_sum = jnp.zeros((W, LANES), f32)
    last_sum = jnp.zeros((W, LANES), f32)
    for g in range(GROUPS):
        lanes = slice(g * LANES, (g + 1) * LANES)
        pull = cot_t[:, lanes] * prefix[:, lanes]
        blend = seg[g, 0]
        slope = seg[g, 2] * (prefix[:, lanes] * seg[g, 1] - tail[:, lanes])
        for s in range(SLOTS):
            at = (g % WIDE) * GROUP + s * LANES
            d_logit = slope[s : s + 1, :]
            grads = pull * blend[s : s + 1, :] + head_col * d_logit
            head_sum = head_sum + feat[g // WIDE, :, at : at + LANES] * d_logit
            last_sum = last_sum + grads
            grad[g // WIDE, :, at : at + LANES] = grads.astype(bf16)
    col_sums[LAYERS] = head_sum
    col_sums[LAYERS - 1] = last_sum

    def phase1(layer, half, d):
        there, device = ray_peer(half, d)
        return pltpu.make_async_remote_copy(
            src_ref=dw.at[
                layer, pl.ds(pl.multiple_of(half * (W // 2) + there * BLOCK, BLOCK), BLOCK), :
            ],
            dst_ref=in1.at[layer, half, d],
            send_sem=sends.at[0, layer, half, d],
            recv_sem=recvs.at[0, layer, half, d],
            device_id=device,
            device_id_type=MESH,
        )

    def phase2(layer, half, d):
        return pltpu.make_async_remote_copy(
            src_ref=red.at[layer, half],
            dst_ref=in2.at[layer, half, spot[1 - half]],
            send_sem=sends.at[1, layer, half, d],
            recv_sem=recvs.at[1, layer, half, d],
            device_id=ray_peer(1 - half, d)[1],
            device_id_type=MESH,
        )

    def own_rows(half):
        return pl.ds(pl.multiple_of(half * (W // 2) + spot[half] * BLOCK, BLOCK), BLOCK)

    def phase3(layer, half, d):
        rows = dw_out.at[layer, own_rows(half), :]
        return pltpu.make_async_remote_copy(
            src_ref=rows,
            dst_ref=rows,
            send_sem=sends.at[2, layer, half, d],
            recv_sem=recvs.at[2, layer, half, d],
            device_id=ray_peer(half, d)[1],
            device_id_type=MESH,
        )

    def small_copy(axis, d):
        return pltpu.make_async_remote_copy(
            src_ref=(small, small_x.at[SIDE])[axis],
            dst_ref=(small_x, small_y)[axis].at[spot[axis]],
            send_sem=small_send.at[axis, d],
            recv_sem=small_recv.at[axis, d],
            device_id=ray_peer(axis, d)[1],
            device_id_type=MESH,
        )

    for layer in range(LAYERS - 1, -1, -1):
        for c in range(CHUNKS):
            if layer > 0:
                term = dot(hid[layer - 1, c], grad[c], 1, 1)
            else:
                term = dot(grad[c], x16[c], 1, 0)
            total = term if c == 0 else total + term
        dw[layer] = total if layer > 0 else total.T
        for d in range(1, SIDE):
            for half in (0, 1):
                phase1(layer, half, d).start()
        if layer > 0:
            def back(c, acc):
                pulled = jnp.where(hid[layer - 1, c] > 0, dot(w[layer], grad[c], 1, 0), 0.0)
                grad[c] = pulled.astype(bf16)
                for t in range(CHUNK // LANES):
                    acc = acc + pulled[:, t * LANES : (t + 1) * LANES]
                return acc

            acc = jnp.zeros((W, LANES), f32)
            for c in range(CHUNKS):
                acc = back(c, acc)
            col_sums[layer - 1] = acc

    lane = lax.broadcasted_iota(jnp.int32, (W, LANES), 1)
    gathered_cols = jnp.zeros((W, LANES), f32)
    for k in range(LAYERS + 1):
        gathered_cols = jnp.where(
            lane == k, jnp.sum(col_sums[k], axis=1, keepdims=True), gathered_cols
        )
    small[...] = gathered_cols.T[:8, :]
    for d in range(1, SIDE):
        small_copy(0, d).start()

    order = range(LAYERS - 1, -1, -1)
    for layer in order:
        for half in (0, 1):
            total = dw[layer, own_rows(half), :]
            for d in range(1, SIDE):
                phase1(layer, half, d).wait_recv()
                total = total + in1[layer, half, d]
            red[layer, half] = total
            in2[layer, half, spot[1 - half]] = total
            for d in range(1, SIDE):
                phase2(layer, half, d).start()

    small_x[spot[0]] = small[...]
    for d in range(1, SIDE):
        small_copy(0, d).wait_recv()
    small_x[SIDE] = (small_x[0] + small_x[1]) + (small_x[2] + small_x[3])
    for d in range(1, SIDE):
        small_copy(1, d).start()

    for layer in order:
        for half in (0, 1):
            for d in range(1, SIDE):
                phase2(layer, half, d).wait_recv()
            total = (in2[layer, half, 0] + in2[layer, half, 1]) + (
                in2[layer, half, 2] + in2[layer, half, 3]
            )
            dw_out[layer, own_rows(half), :] = total
            for d in range(1, SIDE):
                phase3(layer, half, d).start()

    small_y[spot[1]] = small_x[SIDE]
    for d in range(1, SIDE):
        small_copy(1, d).wait_recv()
    summed = (small_y[0] + small_y[1]) + (small_y[2] + small_y[3])
    bias_out[...] = summed[:LAYERS, :]
    head_out[...] = summed[LAYERS : LAYERS + 1, :]

    comp_in[space] = colour_rows[pl.ds(pl.multiple_of(space * kept, kept), kept), :]
    for d in range(1, PARTS):
        comp_copy(d).wait_recv()
    total = comp_in[0]
    for q in range(1, PARTS):
        total = total + comp_in[q]
    comp_out[...] = total

    for layer in order:
        for half in (0, 1):
            for d in range(1, SIDE):
                phase3(layer, half, d).wait_recv()
    for d in range(1, PARTS):
        ag_copy(d).wait_send()
        comp_copy(d).wait_send()
    for axis in (0, 1):
        for d in range(1, SIDE):
            small_copy(axis, d).wait_send()
            for layer in order:
                for phase in (phase1, phase2, phase3):
                    phase(layer, axis, d).wait_send()


def hand_out(*refs):
    sems = refs[8]
    copies = [pltpu.make_async_copy(refs[k], refs[4 + k], sems.at[k]) for k in (1, 0, 2, 3)]
    for copy in copies:
        copy.start()
    for copy in copies:
        copy.wait()


def on_device(
    grid_table, weights, biases, density_head, sample_cells, sample_counts, ray_order, cotangent
):
    cells = sample_cells[0].T.reshape(SLOTS, GROUPS, LANES).transpose(1, 0, 2).reshape(SAMPLES)
    counts = sample_counts.reshape(GROUPS, LANES)
    in_vmem = pl.BlockSpec(memory_space=pltpu.VMEM)
    in_hbm = pl.BlockSpec(memory_space=pl.ANY)
    dma = pltpu.SemaphoreType.DMA
    composite, dw, db, dh = pl.pallas_call(
        kernel,
        out_shape=(
            pltpu.VMEM((RAYS // PARTS, W), f32),
            pltpu.VMEM((LAYERS, W, W), f32),
            pltpu.VMEM((LAYERS, W), f32),
            pltpu.VMEM((1, W), f32),
        ),
        in_specs=[
            pl.BlockSpec(memory_space=pltpu.SMEM), in_hbm, in_hbm, in_vmem, in_vmem, in_vmem, in_vmem, in_hbm
        ],
        out_specs=(in_vmem,) * 4,
        scratch_shapes=[
            pltpu.VMEM((CELLS, W), bf16),
            pltpu.VMEM((LAYERS, W, W), bf16),
            pltpu.VMEM((RAYS, W), f32),
            dma((PIECES + 2,)),
            pltpu.VMEM((2 * CELLS, LANES), f32),
            pltpu.VMEM((2 * SAMPLES, LANES), f32),
            pltpu.VMEM((CHUNKS, CHUNK, W), bf16),
            pltpu.VMEM((LAYERS, W, W), bf16),
            pltpu.VMEM((W, 8), f32),
            pltpu.VMEM((W, RAYS), f32),
            pltpu.VMEM((LAYERS - 1, CHUNKS, W, CHUNK), bf16),
            pltpu.VMEM((CHUNKS, W, CHUNK), f32),
            pltpu.VMEM((CHUNKS, W, CHUNK), bf16),
            pltpu.VMEM((GROUPS, 3, SLOTS, LANES), f32),
            pltpu.VMEM((GROUPS, W, LANES), f32),
            pltpu.VMEM((RAYS, W), f32),
            pltpu.VMEM((8, LANES), f32),
            pltpu.VMEM((PARTS * 8, LANES), f32),
            pltpu.VMEM((PARTS, RAYS // PARTS, W), f32),
            pltpu.VMEM((LAYERS, W, W), f32),
            pltpu.VMEM((LAYERS + 1, W, LANES), f32),
            pltpu.VMEM((8, W), f32),
            pltpu.VMEM((SIDE + 1, 8, W), f32),
            pltpu.VMEM((SIDE, 8, W), f32),
            pltpu.VMEM((LAYERS, 2, BLOCK, W), f32),
            pltpu.VMEM((LAYERS, 2, SIDE, BLOCK, W), f32),
            pltpu.VMEM((LAYERS, 2, SIDE, BLOCK, W), f32),
            dma((PARTS,)),
            dma((PARTS,)),
            dma((PARTS,)),
            dma((PARTS,)),
            dma((3, LAYERS, 2, SIDE)),
            dma((3, LAYERS, 2, SIDE)),
            dma((2, SIDE)),
            dma((2, SIDE)),
        ],
        compiler_params=pltpu.CompilerParams(
            collective_id=0, has_side_effects=True, vmem_limit_bytes=58 << 20
        ),
        cost_estimate=pl.CostEstimate(
            flops=22 * SAMPLES * W * W, bytes_accessed=6 << 20, transcendentals=6 * SAMPLES
        ),
    )(
        cells, grid_table[0], weights[0], biases[0], density_head, counts, ray_order.T, cotangent
    )
    parts = (composite, dw, db, dh)
    composite, dw, db, dh = pl.pallas_call(
        hand_out,
        out_shape=tuple(jax.ShapeDtypeStruct(p.shape, f32) for p in parts),
        in_specs=[in_vmem] * 4,
        out_specs=(pl.BlockSpec(memory_space=pl.ANY),) * 4,
        scratch_shapes=[dma((4,))],
    )(*(pltpu.with_memory_space_constraint(p, pltpu.VMEM) for p in parts))
    return composite, dw[None], db[None], dh


def solution(mesh):
    placed = (
        P("space", None, None),
        P("space", None, None, None),
        P("space", None, None),
        P("space", None),
        P("space", "ray", None),
        P("ray", "space"),
        P("ray", None),
        P("ray", None),
    )
    return jax.shard_map(
        on_device,
        mesh=mesh,
        in_specs=placed,
        out_specs=(
            P(("ray", "space"), None),
            P("space", None, None, None),
            P("space", None, None),
            P("space", None),
        ),
        check_vma=False,
    )
```

```python
import jax
import jax.numpy as jnp
from jax import lax
from jax.experimental import pallas as pl
from jax.experimental.pallas import tpu as pltpu
from jax.sharding import PartitionSpec as P

MESH = pl.DeviceIdType.MESH
f32 = jnp.float32
bf16 = jnp.bfloat16

STEP = 0.05
W = 256
LAYERS = 4
SLOTS = 8
CELLS = 4096
LANES = 128
RAYS = 512
GROUPS = RAYS // LANES
GROUP = SLOTS * LANES
SAMPLES = RAYS * SLOTS
WIDE = 4
CHUNKS = GROUPS // WIDE
CHUNK = WIDE * GROUP
PARTS = 16
SIDE = 4
BLOCK = W // 2 // SIDE
UNROLL = 32


def dot(a, b, ca, cb):
    return lax.dot_general(a, b, (((ca,), (cb,)), ((), ())), preferred_element_type=f32)


def scan_down(v, row):
    for k in (1, 2, 4):
        v = v + jnp.where(row >= k, pltpu.roll(v, k, 0), 0.0)
    return v


def scan_up(v, row):
    for k in (1, 2, 4):
        v = v + jnp.where(row < SLOTS - k, pltpu.roll(v, SLOTS - k, 0), 0.0)
    return v


def kernel(
    cells, table, w, bias, head, counts, ranks, cot,
    comp_out, dw_out, bias_out, head_out,
    table32, rows32, x16, wt, cols, cot_t, hid, feat, grad, seg, colour, colour_rows,
    packed, gathered, comp_in, dw, col_sums, small, small_x, small_y,
    red, in1, in2,
    ag_send, ag_recv, comp_send, comp_recv, sends, recvs, small_send, small_recv,
):
    space = lax.axis_index("space")
    ray = lax.axis_index("ray")
    spot = (ray // SIDE, ray % SIDE)

    def ray_peer(axis, d):
        there = lax.rem(spot[axis] + d, SIDE)
        return there, {"ray": there * SIDE + spot[1] if axis == 0 else spot[0] * SIDE + there}

    barrier = pltpu.get_barrier_semaphore()
    for d in range(1, PARTS):
        pl.semaphore_signal(
            barrier, inc=1, device_id={"space": lax.rem(space + d, PARTS)}, device_id_type=MESH
        )
    for axis in (0, 1):
        for d in range(1, SIDE):
            pl.semaphore_signal(
                barrier, inc=1, device_id=ray_peer(axis, d)[1], device_id_type=MESH
            )

    def widen(k, _):
        part = table[pl.ds(pl.multiple_of(k * 512, 512), 512), :].astype(f32)
        table32[pl.ds(pl.multiple_of(k * 1024, 1024), 512, stride=2), :] = part[:, :LANES]
        table32[pl.ds(pl.multiple_of(k * 1024, 1024) + 1, 512, stride=2), :] = part[:, LANES:]
        return 0

    lax.fori_loop(0, CELLS // 512, widen, 0)

    def pick(k, _):
        base = k * UNROLL
        got = [
            table32[pl.ds(2 * cells[base + u], 2), :] for u in range(UNROLL)
        ]
        for u in range(UNROLL):
            rows32[pl.ds(pl.multiple_of(2 * base, 2 * UNROLL) + 2 * u, 2), :] = got[u]
        return 0

    lax.fori_loop(0, GROUP // UNROLL, pick, 0)

    for layer in range(LAYERS):
        wt[layer] = w[layer].T
    cols[...] = jnp.concatenate([bias[...], head[...], jnp.zeros((3, W), f32)], axis=0).T
    cot_t[...] = cot[...].T
    slot_row = lax.broadcasted_iota(jnp.int32, (SLOTS, LANES), 0)
    ones = jnp.ones((1, LANES), f32)
    head_col = cols[:, LAYERS : LAYERS + 1] * ones

    def forward(g, more):
        start = pl.multiple_of(g * 2 * GROUP, 2 * GROUP)
        low = rows32[pl.ds(start, GROUP, stride=2), :]
        high = rows32[pl.ds(start + 1, GROUP, stride=2), :]
        x = jnp.concatenate([low, high], axis=1).astype(bf16)
        half = pl.ds(pl.multiple_of((g % WIDE) * GROUP, GROUP), GROUP)
        x16[g // WIDE, half, :] = x
        value = None
        for layer in range(LAYERS):
            if more:
                for u in range(layer * GROUP // LAYERS, (layer + 1) * GROUP // LAYERS):
                    row = table32[pl.ds(2 * cells[(g + 1) * GROUP + u], 2), :]
                    rows32[pl.ds(pl.multiple_of((g + 1) * 2 * GROUP, 2 * GROUP) + 2 * u, 2), :] = row
            value = dot(wt[layer], x, 1, 1 if layer == 0 else 0) + cols[:, layer : layer + 1]
            if layer + 1 < LAYERS:
                x = jnp.maximum(value, 0.0).astype(bf16)
                hid[layer, g // WIDE, :, half] = x
        feat[g // WIDE, :, half] = value

    def segment(g):
        turned = cot_t[:, pl.ds(pl.multiple_of(g * LANES, LANES), LANES)]
        logit, along = [], []
        for s in range(SLOTS):
            at = pl.multiple_of((g % WIDE) * GROUP, GROUP) + s * LANES
            f = feat[g // WIDE, :, pl.ds(at, LANES)]
            logit.append(jnp.sum(f * head_col, axis=0, keepdims=True))
            along.append(jnp.sum(f * turned, axis=0, keepdims=True))
        logit = jnp.concatenate(logit, axis=0)
        along = jnp.concatenate(along, axis=0)
        live = slot_row < counts[pl.ds(g, 1), :]
        density = jnp.maximum(logit, 0.0) + jnp.log1p(jnp.exp(-jnp.abs(logit)))
        optical = jnp.where(live, density * STEP, 0.0)
        total = scan_down(optical, slot_row)
        through = jnp.exp(-(total - optical))
        past = jnp.exp(-optical)
        blend = through * (1.0 - past)
        share = blend * along
        after = scan_up(share, slot_row)
        seg[g, 0] = blend
        seg[g, 1] = along * through * past - (after - share)
        seg[g, 2] = jnp.where(live, STEP / (1.0 + jnp.exp(-logit)), 0.0)
        packed[pl.ds(g, 1), :] = -total[SLOTS - 1 : SLOTS, :]
        packed[pl.ds(GROUPS + g, 1), :] = after[0:1, :]

    for g in range(GROUPS):
        forward(g, g + 1 < GROUPS)
        if g > 0:
            segment(g - 1)
    segment(GROUPS - 1)

    pl.semaphore_wait(barrier, PARTS - 1 + 2 * (SIDE - 1))
    mine = pl.multiple_of(space * 8, 8)

    def ag_copy(d):
        return pltpu.make_async_remote_copy(
            src_ref=packed,
            dst_ref=gathered.at[pl.ds(mine, 8), :],
            send_sem=ag_send.at[d],
            recv_sem=ag_recv.at[d],
            device_id={"space": lax.rem(space + d, PARTS)},
            device_id_type=MESH,
        )

    for d in range(1, PARTS):
        ag_copy(d).start()
    gathered[pl.ds(mine, 8), :] = packed[...]

    def blend_colours(g, _):
        c = g // WIDE
        at = pl.multiple_of((g % WIDE) * GROUP, GROUP)
        blend = seg[g, 0]
        acc = None
        for s in range(SLOTS):
            term = feat[c, :, pl.ds(at + s * LANES, LANES)] * blend[s : s + 1, :]
            acc = term if acc is None else acc + term
        colour[g] = acc
        return 0

    lax.fori_loop(0, GROUPS, blend_colours, 0)
    for d in range(1, PARTS):
        ag_copy(d).wait_recv()

    decay = jnp.concatenate(
        [gathered[pl.ds(g, PARTS, stride=8), :] for g in range(GROUPS)], axis=1
    )
    product = jnp.concatenate(
        [gathered[pl.ds(GROUPS + g, PARTS, stride=8), :] for g in range(GROUPS)], axis=1
    )
    rank = ranks[...]
    earlier = jnp.zeros((PARTS, RAYS), f32)
    for q in range(PARTS):
        earlier = earlier + jnp.where(rank[q : q + 1, :] < rank, decay[q : q + 1, :], 0.0)
    prefixes = jnp.exp(earlier)
    own = lax.broadcasted_iota(jnp.int32, (PARTS, RAYS), 0) == space
    own_rank = jnp.sum(jnp.where(own, rank, 0), axis=0, keepdims=True)
    prefix = jnp.sum(jnp.where(own, prefixes, 0.0), axis=0, keepdims=True)
    tail = jnp.sum(jnp.where(rank > own_rank, prefixes * product, 0.0), axis=0, keepdims=True)

    for g in range(GROUPS):
        lanes = slice(g * LANES, (g + 1) * LANES)
        colour_rows[lanes, :] = (colour[g] * prefix[:, lanes]).T
    kept = RAYS // PARTS

    def comp_copy(d):
        there = lax.rem(space + d, PARTS)
        return pltpu.make_async_remote_copy(
            src_ref=colour_rows.at[pl.ds(pl.multiple_of(there * kept, kept), kept), :],
            dst_ref=comp_in.at[space],
            send_sem=comp_send.at[d],
            recv_sem=comp_recv.at[d],
            device_id={"space": there},
            device_id_type=MESH,
        )

    for d in range(1, PARTS):
        comp_copy(d).start()

    head_sum = jnp.zeros((W, LANES), f32)
    last_sum = jnp.zeros((W, LANES), f32)
    for g in range(GROUPS):
        lanes = slice(g * LANES, (g + 1) * LANES)
        pull = cot_t[:, lanes] * prefix[:, lanes]
        blend = seg[g, 0]
        slope = seg[g, 2] * (prefix[:, lanes] * seg[g, 1] - tail[:, lanes])
        for s in range(SLOTS):
            at = (g % WIDE) * GROUP + s * LANES
            d_logit = slope[s : s + 1, :]
            grads = pull * blend[s : s + 1, :] + head_col * d_logit
            head_sum = head_sum + feat[g // WIDE, :, at : at + LANES] * d_logit
            last_sum = last_sum + grads
            grad[g // WIDE, :, at : at + LANES] = grads.astype(bf16)
    col_sums[LAYERS] = head_sum
    col_sums[LAYERS - 1] = last_sum

    def phase1(layer, half, d):
        there, device = ray_peer(half, d)
        return pltpu.make_async_remote_copy(
            src_ref=dw.at[
                layer, pl.ds(pl.multiple_of(half * (W // 2) + there * BLOCK, BLOCK), BLOCK), :
            ],
            dst_ref=in1.at[layer, half, d],
            send_sem=sends.at[0, layer, half, d],
            recv_sem=recvs.at[0, layer, half, d],
            device_id=device,
            device_id_type=MESH,
        )

    def phase2(layer, half, d):
        return pltpu.make_async_remote_copy(
            src_ref=red.at[layer, half],
            dst_ref=in2.at[layer, half, spot[1 - half]],
            send_sem=sends.at[1, layer, half, d],
            recv_sem=recvs.at[1, layer, half, d],
            device_id=ray_peer(1 - half, d)[1],
            device_id_type=MESH,
        )

    def own_rows(half):
        return pl.ds(pl.multiple_of(half * (W // 2) + spot[half] * BLOCK, BLOCK), BLOCK)

    def phase3(layer, half, d):
        rows = dw_out.at[layer, own_rows(half), :]
        return pltpu.make_async_remote_copy(
            src_ref=rows,
            dst_ref=rows,
            send_sem=sends.at[2, layer, half, d],
            recv_sem=recvs.at[2, layer, half, d],
            device_id=ray_peer(half, d)[1],
            device_id_type=MESH,
        )

    def small_copy(axis, d):
        return pltpu.make_async_remote_copy(
            src_ref=(small, small_x.at[SIDE])[axis],
            dst_ref=(small_x, small_y)[axis].at[spot[axis]],
            send_sem=small_send.at[axis, d],
            recv_sem=small_recv.at[axis, d],
            device_id=ray_peer(axis, d)[1],
            device_id_type=MESH,
        )

    for layer in range(LAYERS - 1, -1, -1):
        for c in range(CHUNKS):
            if layer > 0:
                term = dot(hid[layer - 1, c], grad[c], 1, 1)
            else:
                term = dot(grad[c], x16[c], 1, 0)
            total = term if c == 0 else total + term
        dw[layer] = total if layer > 0 else total.T
        for d in range(1, SIDE):
            for half in (0, 1):
                phase1(layer, half, d).start()
        if layer > 0:
            def back(c, acc):
                pulled = jnp.where(hid[layer - 1, c] > 0, dot(w[layer], grad[c], 1, 0), 0.0)
                grad[c] = pulled.astype(bf16)
                for t in range(CHUNK // LANES):
                    acc = acc + pulled[:, t * LANES : (t + 1) * LANES]
                return acc

            acc = jnp.zeros((W, LANES), f32)
            for c in range(CHUNKS):
                acc = back(c, acc)
            col_sums[layer - 1] = acc

    lane = lax.broadcasted_iota(jnp.int32, (W, LANES), 1)
    gathered_cols = jnp.zeros((W, LANES), f32)
    for k in range(LAYERS + 1):
        gathered_cols = jnp.where(
            lane == k, jnp.sum(col_sums[k], axis=1, keepdims=True), gathered_cols
        )
    small[...] = gathered_cols.T[:8, :]
    for d in range(1, SIDE):
        small_copy(0, d).start()

    order = range(LAYERS - 1, -1, -1)
    for layer in order:
        for half in (0, 1):
            total = dw[layer, own_rows(half), :]
            for d in range(1, SIDE):
                phase1(layer, half, d).wait_recv()
                total = total + in1[layer, half, d]
            red[layer, half] = total
            in2[layer, half, spot[1 - half]] = total
            for d in range(1, SIDE):
                phase2(layer, half, d).start()

    small_x[spot[0]] = small[...]
    for d in range(1, SIDE):
        small_copy(0, d).wait_recv()
    small_x[SIDE] = (small_x[0] + small_x[1]) + (small_x[2] + small_x[3])
    for d in range(1, SIDE):
        small_copy(1, d).start()

    for layer in order:
        for half in (0, 1):
            for d in range(1, SIDE):
                phase2(layer, half, d).wait_recv()
            total = (in2[layer, half, 0] + in2[layer, half, 1]) + (
                in2[layer, half, 2] + in2[layer, half, 3]
            )
            dw_out[layer, own_rows(half), :] = total
            for d in range(1, SIDE):
                phase3(layer, half, d).start()

    small_y[spot[1]] = small_x[SIDE]
    for d in range(1, SIDE):
        small_copy(1, d).wait_recv()
    summed = (small_y[0] + small_y[1]) + (small_y[2] + small_y[3])
    bias_out[...] = summed[:LAYERS, :]
    head_out[...] = summed[LAYERS : LAYERS + 1, :]

    comp_in[space] = colour_rows[pl.ds(pl.multiple_of(space * kept, kept), kept), :]
    for d in range(1, PARTS):
        comp_copy(d).wait_recv()
    total = comp_in[0]
    for q in range(1, PARTS):
        total = total + comp_in[q]
    comp_out[...] = total

    for layer in order:
        for half in (0, 1):
            for d in range(1, SIDE):
                phase3(layer, half, d).wait_recv()
    for d in range(1, PARTS):
        ag_copy(d).wait_send()
        comp_copy(d).wait_send()
    for axis in (0, 1):
        for d in range(1, SIDE):
            small_copy(axis, d).wait_send()
            for layer in order:
                for phase in (phase1, phase2, phase3):
                    phase(layer, axis, d).wait_send()


def hand_out(*refs):
    sems = refs[8]
    copies = [pltpu.make_async_copy(refs[k], refs[4 + k], sems.at[k]) for k in (1, 0, 2, 3)]
    for copy in copies:
        copy.start()
    for copy in copies:
        copy.wait()


def on_device(
    grid_table, weights, biases, density_head, sample_cells, sample_counts, ray_order, cotangent
):
    cells = sample_cells[0].T.reshape(SLOTS, GROUPS, LANES).transpose(1, 0, 2).reshape(SAMPLES)
    counts = sample_counts.reshape(GROUPS, LANES)
    in_vmem = pl.BlockSpec(memory_space=pltpu.VMEM)
    dma = pltpu.SemaphoreType.DMA
    composite, dw, db, dh = pl.pallas_call(
        kernel,
        out_shape=(
            pltpu.VMEM((RAYS // PARTS, W), f32),
            pltpu.VMEM((LAYERS, W, W), f32),
            pltpu.VMEM((LAYERS, W), f32),
            pltpu.VMEM((1, W), f32),
        ),
        in_specs=[pl.BlockSpec(memory_space=pltpu.SMEM)] + [in_vmem] * 7,
        out_specs=(in_vmem,) * 4,
        scratch_shapes=[
            pltpu.VMEM((2 * CELLS, LANES), f32),
            pltpu.VMEM((2 * SAMPLES, LANES), f32),
            pltpu.VMEM((CHUNKS, CHUNK, W), bf16),
            pltpu.VMEM((LAYERS, W, W), bf16),
            pltpu.VMEM((W, 8), f32),
            pltpu.VMEM((W, RAYS), f32),
            pltpu.VMEM((LAYERS - 1, CHUNKS, W, CHUNK), bf16),
            pltpu.VMEM((CHUNKS, W, CHUNK), f32),
            pltpu.VMEM((CHUNKS, W, CHUNK), bf16),
            pltpu.VMEM((GROUPS, 3, SLOTS, LANES), f32),
            pltpu.VMEM((GROUPS, W, LANES), f32),
            pltpu.VMEM((RAYS, W), f32),
            pltpu.VMEM((8, LANES), f32),
            pltpu.VMEM((PARTS * 8, LANES), f32),
            pltpu.VMEM((PARTS, RAYS // PARTS, W), f32),
            pltpu.VMEM((LAYERS, W, W), f32),
            pltpu.VMEM((LAYERS + 1, W, LANES), f32),
            pltpu.VMEM((8, W), f32),
            pltpu.VMEM((SIDE + 1, 8, W), f32),
            pltpu.VMEM((SIDE, 8, W), f32),
            pltpu.VMEM((LAYERS, 2, BLOCK, W), f32),
            pltpu.VMEM((LAYERS, 2, SIDE, BLOCK, W), f32),
            pltpu.VMEM((LAYERS, 2, SIDE, BLOCK, W), f32),
            dma((PARTS,)),
            dma((PARTS,)),
            dma((PARTS,)),
            dma((PARTS,)),
            dma((3, LAYERS, 2, SIDE)),
            dma((3, LAYERS, 2, SIDE)),
            dma((2, SIDE)),
            dma((2, SIDE)),
        ],
        compiler_params=pltpu.CompilerParams(
            collective_id=0, has_side_effects=True, vmem_limit_bytes=58 << 20
        ),
        cost_estimate=pl.CostEstimate(
            flops=22 * SAMPLES * W * W, bytes_accessed=6 << 20, transcendentals=6 * SAMPLES
        ),
    )(
        cells, grid_table[0], weights[0], biases[0], density_head, counts, ray_order.T, cotangent
    )
    parts = (composite, dw, db, dh)
    composite, dw, db, dh = pl.pallas_call(
        hand_out,
        out_shape=tuple(jax.ShapeDtypeStruct(p.shape, f32) for p in parts),
        in_specs=[in_vmem] * 4,
        out_specs=(pl.BlockSpec(memory_space=pl.ANY),) * 4,
        scratch_shapes=[dma((4,))],
    )(*(pltpu.with_memory_space_constraint(p, pltpu.VMEM) for p in parts))
    return composite, dw[None], db[None], dh


def solution(mesh):
    placed = (
        P("space", None, None),
        P("space", None, None, None),
        P("space", None, None),
        P("space", None),
        P("space", "ray", None),
        P("ray", "space"),
        P("ray", None),
        P("ray", None),
    )
    return jax.shard_map(
        on_device,
        mesh=mesh,
        in_specs=placed,
        out_specs=(
            P(("ray", "space"), None),
            P("space", None, None, None),
            P("space", None, None),
            P("space", None),
        ),
        check_vma=False,
    )
```

```python
import jax
import jax.numpy as jnp
from jax import lax
from jax.experimental import pallas as pl
from jax.experimental.pallas import tpu as pltpu
from jax.sharding import PartitionSpec as P

MESH = pl.DeviceIdType.MESH
f32 = jnp.float32
bf16 = jnp.bfloat16

STEP = 0.05
W = 256
LAYERS = 4
SLOTS = 8
CELLS = 4096
LANES = 128
RAYS = 512
GROUPS = RAYS // LANES
GROUP = SLOTS * LANES
SAMPLES = RAYS * SLOTS
WIDE = 4
CHUNKS = GROUPS // WIDE
CHUNK = WIDE * GROUP
PARTS = 16
SIDE = 4
BLOCK = W // 2 // SIDE
UNROLL = 32


def dot(a, b, ca, cb):
    return lax.dot_general(a, b, (((ca,), (cb,)), ((), ())), preferred_element_type=f32)


def scan_down(v, row):
    for k in (1, 2, 4):
        v = v + jnp.where(row >= k, pltpu.roll(v, k, 0), 0.0)
    return v


def scan_up(v, row):
    for k in (1, 2, 4):
        v = v + jnp.where(row < SLOTS - k, pltpu.roll(v, SLOTS - k, 0), 0.0)
    return v


def kernel(
    cells, table, w, bias, head, counts, ranks, cot,
    comp_out, dw_out, bias_out, head_out,
    table32, rows32, x16, wt, cols, cot_t, hid, feat, grad, seg, colour, colour_rows,
    packed, gathered, comp_in, dw, col_sums, small, small_x, small_y,
    red, in1, in2,
    ag_send, ag_recv, comp_send, comp_recv, sends, recvs, small_send, small_recv,
):
    space = lax.axis_index("space")
    ray = lax.axis_index("ray")
    spot = (ray // SIDE, ray % SIDE)

    def ray_peer(axis, d):
        there = lax.rem(spot[axis] + d, SIDE)
        return there, {"ray": there * SIDE + spot[1] if axis == 0 else spot[0] * SIDE + there}

    barrier = pltpu.get_barrier_semaphore()
    for d in range(1, PARTS):
        pl.semaphore_signal(
            barrier, inc=1, device_id={"space": lax.rem(space + d, PARTS)}, device_id_type=MESH
        )
    for axis in (0, 1):
        for d in range(1, SIDE):
            pl.semaphore_signal(
                barrier, inc=1, device_id=ray_peer(axis, d)[1], device_id_type=MESH
            )

    def widen(k, _):
        part = table[pl.ds(pl.multiple_of(k * 512, 512), 512), :].astype(f32)
        table32[pl.ds(pl.multiple_of(k * 1024, 1024), 512, stride=2), :] = part[:, :LANES]
        table32[pl.ds(pl.multiple_of(k * 1024, 1024) + 1, 512, stride=2), :] = part[:, LANES:]
        return 0

    lax.fori_loop(0, CELLS // 512, widen, 0)

    def pick(k, _):
        base = k * UNROLL
        got = [
            table32[pl.ds(2 * cells[base + u], 2), :] for u in range(UNROLL)
        ]
        for u in range(UNROLL):
            rows32[pl.ds(pl.multiple_of(2 * base, 2 * UNROLL) + 2 * u, 2), :] = got[u]
        return 0

    lax.fori_loop(0, GROUP // UNROLL, pick, 0)

    for layer in range(LAYERS):
        wt[layer] = w[layer].T
    cols[...] = jnp.concatenate([bias[...], head[...], jnp.zeros((3, W), f32)], axis=0).T
    cot_t[...] = cot[...].T
    slot_row = lax.broadcasted_iota(jnp.int32, (SLOTS, LANES), 0)
    ones = jnp.ones((1, LANES), f32)
    head_col = cols[:, LAYERS : LAYERS + 1] * ones

    def forward(g, more):
        start = pl.multiple_of(g * 2 * GROUP, 2 * GROUP)
        low = rows32[pl.ds(start, GROUP, stride=2), :]
        high = rows32[pl.ds(start + 1, GROUP, stride=2), :]
        x = jnp.concatenate([low, high], axis=1).astype(bf16)
        half = pl.ds(pl.multiple_of((g % WIDE) * GROUP, GROUP), GROUP)
        x16[g // WIDE, half, :] = x
        value = None
        for layer in range(LAYERS):
            if more:
                for u in range(layer * GROUP // LAYERS, (layer + 1) * GROUP // LAYERS):
                    row = table32[pl.ds(2 * cells[(g + 1) * GROUP + u], 2), :]
                    rows32[pl.ds(pl.multiple_of((g + 1) * 2 * GROUP, 2 * GROUP) + 2 * u, 2), :] = row
            value = dot(wt[layer], x, 1, 1 if layer == 0 else 0) + cols[:, layer : layer + 1]
            if layer + 1 < LAYERS:
                x = jnp.maximum(value, 0.0).astype(bf16)
                hid[layer, g // WIDE, :, half] = x
        feat[g // WIDE, :, half] = value

    def segment(g):
        turned = cot_t[:, pl.ds(pl.multiple_of(g * LANES, LANES), LANES)]
        logit, along = [], []
        for s in range(SLOTS):
            at = pl.multiple_of((g % WIDE) * GROUP, GROUP) + s * LANES
            f = feat[g // WIDE, :, pl.ds(at, LANES)]
            logit.append(jnp.sum(f * head_col, axis=0, keepdims=True))
            along.append(jnp.sum(f * turned, axis=0, keepdims=True))
        logit = jnp.concatenate(logit, axis=0)
        along = jnp.concatenate(along, axis=0)
        live = slot_row < counts[pl.ds(g, 1), :]
        density = jnp.maximum(logit, 0.0) + jnp.log1p(jnp.exp(-jnp.abs(logit)))
        optical = jnp.where(live, density * STEP, 0.0)
        total = scan_down(optical, slot_row)
        through = jnp.exp(-(total - optical))
        past = jnp.exp(-optical)
        blend = through * (1.0 - past)
        share = blend * along
        after = scan_up(share, slot_row)
        seg[g, 0] = blend
        seg[g, 1] = along * through * past - (after - share)
        seg[g, 2] = jnp.where(live, STEP / (1.0 + jnp.exp(-logit)), 0.0)
        packed[pl.ds(g, 1), :] = -total[SLOTS - 1 : SLOTS, :]
        packed[pl.ds(GROUPS + g, 1), :] = after[0:1, :]

    for g in range(GROUPS):
        forward(g, g + 1 < GROUPS)
        if g > 0:
            segment(g - 1)
    segment(GROUPS - 1)

    pl.semaphore_wait(barrier, PARTS - 1 + 2 * (SIDE - 1))
    mine = pl.multiple_of(space * 8, 8)

    def ag_copy(d):
        return pltpu.make_async_remote_copy(
            src_ref=packed,
            dst_ref=gathered.at[pl.ds(mine, 8), :],
            send_sem=ag_send.at[d],
            recv_sem=ag_recv.at[d],
            device_id={"space": lax.rem(space + d, PARTS)},
            device_id_type=MESH,
        )

    for d in range(1, PARTS):
        ag_copy(d).start()
    gathered[pl.ds(mine, 8), :] = packed[...]

    def blend_colours(g, _):
        c = g // WIDE
        at = pl.multiple_of((g % WIDE) * GROUP, GROUP)
        blend = seg[g, 0]
        acc = None
        for s in range(SLOTS):
            term = feat[c, :, pl.ds(at + s * LANES, LANES)] * blend[s : s + 1, :]
            acc = term if acc is None else acc + term
        colour[g] = acc
        return 0

    lax.fori_loop(0, GROUPS, blend_colours, 0)
    for d in range(1, PARTS):
        ag_copy(d).wait_recv()

    decay = jnp.concatenate(
        [gathered[pl.ds(g, PARTS, stride=8), :] for g in range(GROUPS)], axis=1
    )
    product = jnp.concatenate(
        [gathered[pl.ds(GROUPS + g, PARTS, stride=8), :] for g in range(GROUPS)], axis=1
    )
    rank = ranks[...]
    earlier = jnp.zeros((PARTS, RAYS), f32)
    for q in range(PARTS):
        earlier = earlier + jnp.where(rank[q : q + 1, :] < rank, decay[q : q + 1, :], 0.0)
    prefixes = jnp.exp(earlier)
    own = lax.broadcasted_iota(jnp.int32, (PARTS, RAYS), 0) == space
    own_rank = jnp.sum(jnp.where(own, rank, 0), axis=0, keepdims=True)
    prefix = jnp.sum(jnp.where(own, prefixes, 0.0), axis=0, keepdims=True)
    tail = jnp.sum(jnp.where(rank > own_rank, prefixes * product, 0.0), axis=0, keepdims=True)

    for g in range(GROUPS):
        lanes = slice(g * LANES, (g + 1) * LANES)
        colour_rows[lanes, :] = (colour[g] * prefix[:, lanes]).T
    kept = RAYS // PARTS

    def comp_copy(d):
        there = lax.rem(space + d, PARTS)
        return pltpu.make_async_remote_copy(
            src_ref=colour_rows.at[pl.ds(pl.multiple_of(there * kept, kept), kept), :],
            dst_ref=comp_in.at[space],
            send_sem=comp_send.at[d],
            recv_sem=comp_recv.at[d],
            device_id={"space": there},
            device_id_type=MESH,
        )

    for d in range(1, PARTS):
        comp_copy(d).start()

    head_sum = jnp.zeros((W, LANES), f32)
    last_sum = jnp.zeros((W, LANES), f32)
    for g in range(GROUPS):
        lanes = slice(g * LANES, (g + 1) * LANES)
        pull = cot_t[:, lanes] * prefix[:, lanes]
        blend = seg[g, 0]
        slope = seg[g, 2] * (prefix[:, lanes] * seg[g, 1] - tail[:, lanes])
        for s in range(SLOTS):
            at = (g % WIDE) * GROUP + s * LANES
            d_logit = slope[s : s + 1, :]
            grads = pull * blend[s : s + 1, :] + head_col * d_logit
            head_sum = head_sum + feat[g // WIDE, :, at : at + LANES] * d_logit
            last_sum = last_sum + grads
            grad[g // WIDE, :, at : at + LANES] = grads.astype(bf16)
    col_sums[LAYERS] = head_sum
    col_sums[LAYERS - 1] = last_sum

    def phase1(layer, half, d):
        there, device = ray_peer(half, d)
        return pltpu.make_async_remote_copy(
            src_ref=dw.at[
                layer, pl.ds(pl.multiple_of(half * (W // 2) + there * BLOCK, BLOCK), BLOCK), :
            ],
            dst_ref=in1.at[layer, half, d],
            send_sem=sends.at[0, layer, half, d],
            recv_sem=recvs.at[0, layer, half, d],
            device_id=device,
            device_id_type=MESH,
        )

    def phase2(layer, half, d):
        return pltpu.make_async_remote_copy(
            src_ref=red.at[layer, half],
            dst_ref=in2.at[layer, half, spot[1 - half]],
            send_sem=sends.at[1, layer, half, d],
            recv_sem=recvs.at[1, layer, half, d],
            device_id=ray_peer(1 - half, d)[1],
            device_id_type=MESH,
        )

    def own_rows(half):
        return pl.ds(pl.multiple_of(half * (W // 2) + spot[half] * BLOCK, BLOCK), BLOCK)

    def phase3(layer, half, d):
        rows = dw_out.at[layer, own_rows(half), :]
        return pltpu.make_async_remote_copy(
            src_ref=rows,
            dst_ref=rows,
            send_sem=sends.at[2, layer, half, d],
            recv_sem=recvs.at[2, layer, half, d],
            device_id=ray_peer(half, d)[1],
            device_id_type=MESH,
        )

    def small_copy(axis, d):
        return pltpu.make_async_remote_copy(
            src_ref=(small, small_x.at[SIDE])[axis],
            dst_ref=(small_x, small_y)[axis].at[spot[axis]],
            send_sem=small_send.at[axis, d],
            recv_sem=small_recv.at[axis, d],
            device_id=ray_peer(axis, d)[1],
            device_id_type=MESH,
        )

    for layer in range(LAYERS - 1, -1, -1):
        for c in range(CHUNKS):
            if layer > 0:
                term = dot(hid[layer - 1, c], grad[c], 1, 1)
            else:
                term = dot(grad[c], x16[c], 1, 0)
            total = term if c == 0 else total + term
        dw[layer] = total if layer > 0 else total.T
        for d in range(1, SIDE):
            for half in (0, 1):
                phase1(layer, half, d).start()
        if layer > 0:
            def back(c, acc):
                pulled = jnp.where(hid[layer - 1, c] > 0, dot(w[layer], grad[c], 1, 0), 0.0)
                grad[c] = pulled.astype(bf16)
                for t in range(CHUNK // LANES):
                    acc = acc + pulled[:, t * LANES : (t + 1) * LANES]
                return acc

            acc = jnp.zeros((W, LANES), f32)
            for c in range(CHUNKS):
                acc = back(c, acc)
            col_sums[layer - 1] = acc

    order = range(LAYERS - 1, -1, -1)
    for layer in order:
        if layer == 0:
            lane = lax.broadcasted_iota(jnp.int32, (W, LANES), 1)
            gathered_cols = jnp.zeros((W, LANES), f32)
            for k in range(LAYERS + 1):
                gathered_cols = jnp.where(
                    lane == k, jnp.sum(col_sums[k], axis=1, keepdims=True), gathered_cols
                )
            small[...] = gathered_cols.T[:8, :]
            for d in range(1, SIDE):
                small_copy(0, d).start()
        for half in (0, 1):
            total = dw[layer, own_rows(half), :]
            for d in range(1, SIDE):
                phase1(layer, half, d).wait_recv()
                total = total + in1[layer, half, d]
            red[layer, half] = total
            in2[layer, half, spot[1 - half]] = total
            for d in range(1, SIDE):
                phase2(layer, half, d).start()

    small_x[spot[0]] = small[...]
    for d in range(1, SIDE):
        small_copy(0, d).wait_recv()
    small_x[SIDE] = (small_x[0] + small_x[1]) + (small_x[2] + small_x[3])
    for d in range(1, SIDE):
        small_copy(1, d).start()

    for layer in order:
        for half in (0, 1):
            for d in range(1, SIDE):
                phase2(layer, half, d).wait_recv()
            total = (in2[layer, half, 0] + in2[layer, half, 1]) + (
                in2[layer, half, 2] + in2[layer, half, 3]
            )
            dw_out[layer, own_rows(half), :] = total
            for d in range(1, SIDE):
                phase3(layer, half, d).start()

    small_y[spot[1]] = small_x[SIDE]
    for d in range(1, SIDE):
        small_copy(1, d).wait_recv()
    summed = (small_y[0] + small_y[1]) + (small_y[2] + small_y[3])
    bias_out[...] = summed[:LAYERS, :]
    head_out[...] = summed[LAYERS : LAYERS + 1, :]

    comp_in[space] = colour_rows[pl.ds(pl.multiple_of(space * kept, kept), kept), :]
    for d in range(1, PARTS):
        comp_copy(d).wait_recv()
    total = comp_in[0]
    for q in range(1, PARTS):
        total = total + comp_in[q]
    comp_out[...] = total

    for layer in order:
        for half in (0, 1):
            for d in range(1, SIDE):
                phase3(layer, half, d).wait_recv()
    for d in range(1, PARTS):
        ag_copy(d).wait_send()
        comp_copy(d).wait_send()
    for axis in (0, 1):
        for d in range(1, SIDE):
            small_copy(axis, d).wait_send()
            for layer in order:
                for phase in (phase1, phase2, phase3):
                    phase(layer, axis, d).wait_send()


def hand_out(*refs):
    sems = refs[8]
    copies = [pltpu.make_async_copy(refs[k], refs[4 + k], sems.at[k]) for k in (1, 0, 2, 3)]
    for copy in copies:
        copy.start()
    for copy in copies:
        copy.wait()


def on_device(
    grid_table, weights, biases, density_head, sample_cells, sample_counts, ray_order, cotangent
):
    cells = sample_cells[0].T.reshape(SLOTS, GROUPS, LANES).transpose(1, 0, 2).reshape(SAMPLES)
    counts = sample_counts.reshape(GROUPS, LANES)
    in_vmem = pl.BlockSpec(memory_space=pltpu.VMEM)
    dma = pltpu.SemaphoreType.DMA
    composite, dw, db, dh = pl.pallas_call(
        kernel,
        out_shape=(
            pltpu.VMEM((RAYS // PARTS, W), f32),
            pltpu.VMEM((LAYERS, W, W), f32),
            pltpu.VMEM((LAYERS, W), f32),
            pltpu.VMEM((1, W), f32),
        ),
        in_specs=[pl.BlockSpec(memory_space=pltpu.SMEM)] + [in_vmem] * 7,
        out_specs=(in_vmem,) * 4,
        scratch_shapes=[
            pltpu.VMEM((2 * CELLS, LANES), f32),
            pltpu.VMEM((2 * SAMPLES, LANES), f32),
            pltpu.VMEM((CHUNKS, CHUNK, W), bf16),
            pltpu.VMEM((LAYERS, W, W), bf16),
            pltpu.VMEM((W, 8), f32),
            pltpu.VMEM((W, RAYS), f32),
            pltpu.VMEM((LAYERS - 1, CHUNKS, W, CHUNK), bf16),
            pltpu.VMEM((CHUNKS, W, CHUNK), f32),
            pltpu.VMEM((CHUNKS, W, CHUNK), bf16),
            pltpu.VMEM((GROUPS, 3, SLOTS, LANES), f32),
            pltpu.VMEM((GROUPS, W, LANES), f32),
            pltpu.VMEM((RAYS, W), f32),
            pltpu.VMEM((8, LANES), f32),
            pltpu.VMEM((PARTS * 8, LANES), f32),
            pltpu.VMEM((PARTS, RAYS // PARTS, W), f32),
            pltpu.VMEM((LAYERS, W, W), f32),
            pltpu.VMEM((LAYERS + 1, W, LANES), f32),
            pltpu.VMEM((8, W), f32),
            pltpu.VMEM((SIDE + 1, 8, W), f32),
            pltpu.VMEM((SIDE, 8, W), f32),
            pltpu.VMEM((LAYERS, 2, BLOCK, W), f32),
            pltpu.VMEM((LAYERS, 2, SIDE, BLOCK, W), f32),
            pltpu.VMEM((LAYERS, 2, SIDE, BLOCK, W), f32),
            dma((PARTS,)),
            dma((PARTS,)),
            dma((PARTS,)),
            dma((PARTS,)),
            dma((3, LAYERS, 2, SIDE)),
            dma((3, LAYERS, 2, SIDE)),
            dma((2, SIDE)),
            dma((2, SIDE)),
        ],
        compiler_params=pltpu.CompilerParams(
            collective_id=0, has_side_effects=True, vmem_limit_bytes=58 << 20
        ),
        cost_estimate=pl.CostEstimate(
            flops=22 * SAMPLES * W * W, bytes_accessed=6 << 20, transcendentals=6 * SAMPLES
        ),
    )(
        cells, grid_table[0], weights[0], biases[0], density_head, counts, ray_order.T, cotangent
    )
    parts = (composite, dw, db, dh)
    composite, dw, db, dh = pl.pallas_call(
        hand_out,
        out_shape=tuple(jax.ShapeDtypeStruct(p.shape, f32) for p in parts),
        in_specs=[in_vmem] * 4,
        out_specs=(pl.BlockSpec(memory_space=pl.ANY),) * 4,
        scratch_shapes=[dma((4,))],
    )(*(pltpu.with_memory_space_constraint(p, pltpu.VMEM) for p in parts))
    return composite, dw[None], db[None], dh


def solution(mesh):
    placed = (
        P("space", None, None),
        P("space", None, None, None),
        P("space", None, None),
        P("space", None),
        P("space", "ray", None),
        P("ray", "space"),
        P("ray", None),
        P("ray", None),
    )
    return jax.shard_map(
        on_device,
        mesh=mesh,
        in_specs=placed,
        out_specs=(
            P(("ray", "space"), None),
            P("space", None, None, None),
            P("space", None, None),
            P("space", None),
        ),
        check_vma=False,
    )
```
